512 devices in a mesh: tm: 8 (over x, z_lo), lat: 64 (over z_hi, y, core).
Axes of the slice: x: 4, y: 8, z: 8 (z_hi: 4, z_lo: 2; z = z_hi * 2 + z_lo), core: 2. Of those that a mesh axis runs over, the one named last changes fastest.
Arguments:
- lam: float32 [8, 128, 216, 256], P('tm', 'lat'), may hold values from -6 to 6
- incr: float32 [8, 128, 216, 256], P('tm', 'lat'), may hold values from -6 to 6
- winds: float32 [8, 4, 128, 256], P('tm', None, 'lat'), may hold values from 0.02 to 0.2
- mixing: float32 [8, 216, 216], P('tm'), may hold values from -0.2 to 1
- spread: float32 [8, 128, 216, 256], P('tm', 'lat'), may hold values from 0.3 to 3
- vert_corr: float32 [216, 216], replicated, may hold values from -0.2 to 1
- members: bfloat16 [8, 128, 4, 216, 256], P('tm', 'lat'), may hold values from -6 to 6
Outputs:
- lam_out: float32 [8, 128, 216, 256], P('tm', 'lat')
- incr_out: float32 [8, 128, 216, 256], P('tm', 'lat')
The draws below stay inside these ranges and needn't reach their ends.
All inputs are finite; a program needn't handle non-finite values.
Results may differ from the reference program's by a relative error of at most 0.0027.
Values may be sent and summed in bfloat16 or wider, within the bound.
A program may use at most 64 MiB of HBM per device.

```python
import math
import jax
import jax.numpy as jnp
from jax import lax

COMP = 216
LON = 256
NENS = 4
STEPS = 2
SUBWIN = 8
NLAT = 128


def column_matrix(key, count, leading, diag_level, noise_factor):
    if leading > 0:
        shape = (leading, count, count)
    else:
        shape = (count, count)
    noise_level = noise_factor / count ** 0.5
    noise = jax.random.normal(key, shape, jnp.float32)
    identity = jnp.eye(count, dtype=jnp.float32)
    diagonal = jnp.minimum(diag_level + noise_level * noise, 1.0)
    offdiag = jnp.clip(noise_level * noise, -0.2, 1.0)
    return identity * diagonal + (1.0 - identity) * offdiag


def draw_mixing(key, part):
    key = jax.random.fold_in(key, 11)
    return column_matrix(key, COMP, SUBWIN, 0.8, 0.25)


def draw_vert_corr(key, part):
    key = jax.random.fold_in(key, 12)
    return column_matrix(key, COMP, 0, 0.7, 0.3)


def levels(stream_key, shape, cuts, least, largest):
    def one(axis_at, shards_of):
        draws = jax.random.uniform(jax.random.fold_in(jax.random.fold_in(stream_key, 6), axis_at), (shards_of,), jnp.float32, least / len(cuts), largest / len(cuts))
        return jnp.repeat(jnp.exp(draws), shape[axis_at] // shards_of).reshape((-1,) + (1,) * (len(shape) - axis_at - 1))

    factor_of = one(*cuts[0])
    for cut in cuts[1:]:
        factor_of = factor_of * one(*cut)
    return factor_of


def gaussian(rng, shape, deviation, limit, cuts=(), held_as=jnp.bfloat16):
    loudness = levels(rng, shape, cuts, -0.22, 0.18) if cuts else 1.0
    array = jax.random.normal(rng, shape, jnp.float32) * deviation * loudness
    return jnp.minimum(jnp.maximum(array, -limit), limit).astype(held_as)


def setup_inputs(seed: int = 0) -> dict:
    streams_of = jax.random.split(jax.random.key(seed), 8)
    lam = gaussian(streams_of[0], (SUBWIN, NLAT, COMP, LON), 1.0, 6.0, ((0, 8), (1, 64)), jnp.float32)
    incr = gaussian(streams_of[1], (SUBWIN, NLAT, COMP, LON), 1.0, 6.0, ((0, 8), (1, 64)), jnp.float32)
    winds = jnp.clip(0.02 + 0.18 * jax.random.uniform(streams_of[2], (SUBWIN, 4, NLAT, LON), jnp.float32) ** levels(streams_of[2], (SUBWIN, 4, NLAT, LON), ((0, 8), (2, 64)), -0.2, 0.2), 0.02, 0.2)
    mixing = draw_mixing(jax.random.fold_in(streams_of[7], 71), 0)
    spread = jnp.clip(jnp.exp(math.log(3.0) - 2.3025851 * jax.random.uniform(streams_of[4], (SUBWIN, NLAT, COMP, LON), jnp.float32) ** levels(streams_of[4], (SUBWIN, NLAT, COMP, LON), ((0, 8), (1, 64)), -0.2, 0.2)), 0.3, 3.0)
    vert_corr = draw_vert_corr(jax.random.fold_in(streams_of[7], 71), 0)
    members = gaussian(streams_of[6], (SUBWIN, NLAT, NENS, COMP, LON), 1.0, 6.0, ((0, 8), (1, 64)))
    return dict(lam=lam, incr=incr, winds=winds, mixing=mixing, spread=spread, vert_corr=vert_corr, members=members)


def pad_rows(field_in):
    widths = [(1, 1)] + [(0, 0)] * (field_in.ndim - 1)
    return jnp.pad(field_in, widths)

def smooth(field_in):
    padded = pad_rows(field_in)
    return field_in + 0.25 * (padded[2:] + padded[:-2] + jnp.roll(field_in, -1, -1) + jnp.roll(field_in, 1, -1))

def forward_step(field_in, winds_now, mixer):
    padded = pad_rows(field_in)
    north = winds_now[0][:, None, :]
    south = winds_now[1][:, None, :]
    east = winds_now[2][:, None, :]
    west = winds_now[3][:, None, :]
    centre = 1.0 - north - south - east - west
    combined = centre * field_in + north * padded[2:] + south * padded[:-2]
    combined = combined + east * jnp.roll(field_in, -1, 2) + west * jnp.roll(field_in, 1, 2)
    return jnp.einsum('ab,rbl->ral', mixer, combined, precision=lax.Precision.HIGHEST)

def propagate(field_in, winds_now, mixer):
    for section in range(STEPS):
        field_in = forward_step(field_in, winds_now, mixer)
    return field_in

def covariance(field_in, spread_now, vertical, members_now):
    scaled = spread_now * field_in
    turned = jnp.einsum('ba,rbl->ral', vertical, scaled, precision=lax.Precision.HIGHEST)
    smoothed = smooth(smooth(turned))
    clim = spread_now * jnp.einsum('ab,rbl->ral', vertical, smoothed, precision=lax.Precision.HIGHEST)
    perturb = members_now.astype(jnp.float32)
    weighted = smooth(perturb * field_in[:, None])
    ens = lax.optimization_barrier(jnp.sum(perturb * weighted, axis=1)) / (NENS - 1)
    return 0.5 * clim + 0.5 * ens

def reference(lam, incr, winds, mixing, spread, vert_corr, members):
    first_rows = []
    second_rows = []
    for index in range(SUBWIN):
        term = covariance(lam[index], spread[index], vert_corr, members[index]) + incr[index]
        if index > 0:
            term = term - propagate(incr[index - 1], winds[index - 1], mixing[index - 1])
        first_rows.append(term)
        dual = lam[index]
        if index + 1 < SUBWIN:
            winds_now = winds[index]
            mixer = mixing[index]
            primal, pullback = jax.vjp(lambda state: propagate(state, winds_now, mixer), lam[index + 1])
            dual = dual - pullback(lam[index + 1])[0]
        second_rows.append(dual)
    return (jnp.stack(first_rows), jnp.stack(second_rows))
```

```python
import jax
import jax.numpy as jnp
from jax import lax
from jax.experimental import pallas as pl
from jax.experimental.pallas import tpu as pltpu
from jax.sharding import PartitionSpec as P

MESH = pl.DeviceIdType.MESH
F32, BF16 = jnp.float32, jnp.bfloat16
COMP, LON, NENS = 216, 256, 4
TM, LAT, BAND = 8, 64, 16
CHUNKS = [(at, min(32, COMP - at)) for at in range(0, COMP, 32)]

WIN, INC, SCA, LNX, QEN = 0, 1, 3, 5, 7
ITEMS = 11
ROUTED = (SCA, SCA + 1, QEN + 1, QEN + 2, QEN + 3)


def split(value):
    high = value.astype(BF16)
    return high, (value - high.astype(F32)).astype(BF16)


def dot(a, b):
    return jnp.dot(a, b, preferred_element_type=F32)


def product(mats, base, value):
    high, low = split(value)
    return dot(mats[base], high) + (dot(mats[base + 1], high) + dot(mats[base], low))


def product_16(mats, base, value):
    return dot(mats[base], value) + dot(mats[base + 1], value)


def east_of(value):
    return pltpu.roll(value, LON - 1, 1)


def west_of(value):
    return pltpu.roll(value, 1, 1)


def kernel(
    lam, incr, winds, mixing, spread, vert, members, lam_out, incr_out,
    i6, l6, s6, w3, q_send, q_recv, lam_send, prop_send, arrived, fwd,
    mats, scaled, za, zb, ens,
    tm_send, tm_recv, up_send, up_recv, dn_send, dn_recv, f_in, f_out,
):
    tm, lat = lax.axis_index("tm"), lax.axis_index("lat")
    place = lax.rem(lat, BAND)
    has_up, has_dn = lat < LAT - 1, lat > 0
    has_next, has_prev = tm < TM - 1, tm > 0
    cross_up = (place == BAND - 1) & has_up
    cross_dn = (place == 0) & has_dn
    fwd_up = (place == BAND - 2) & (lat >= BAND)
    fwd_dn = (place == 1) & (lat < LAT - BAND)

    barrier = pltpu.get_barrier_semaphore()
    greetings = (
        (has_next, {"tm": tm + 1}),
        (has_prev, {"tm": tm - 1}),
        (has_up, {"lat": lat + 1}),
        (has_dn, {"lat": lat - 1}),
        (cross_up, {"lat": lat - (BAND - 2)}),
        (cross_dn, {"lat": lat + (BAND - 2)}),
        (fwd_up, {"lat": lat - (BAND - 1)}),
        (fwd_dn, {"lat": lat + (BAND - 1)}),
    )
    targets = 0
    for cond, where in greetings:
        targets = targets + jnp.where(cond, 1, 0)

        @pl.when(cond)
        def _():
            pl.semaphore_signal(barrier, inc=1, device_id=where, device_id_type=MESH)

    def ends(item, up):
        if item == WIN:
            return w3.at[1], w3.at[0 if up else 2]
        for first, buffer in ((INC, i6), (SCA, s6), (LNX, l6)):
            if first <= item < first + 2:
                row = item - first
                return buffer.at[2 + row], buffer.at[row if up else 4 + row]
        m = item - QEN
        return q_send.at[1 if up else 0, m], q_recv.at[0 if up else 1, m]

    def to_lat(item, up):
        src, dst = ends(item, up)
        send, recv = (up_send, up_recv) if up else (dn_send, dn_recv)
        where = {"lat": lat + 1 if up else lat - 1}
        return pltpu.make_async_remote_copy(
            src, dst, send.at[item], recv.at[item], device_id=where, device_id_type=MESH
        )

    def to_fwd(item, up):
        src, _ = ends(item, up)
        at = ROUTED.index(item)
        send = up_send if up else dn_send
        where = {"lat": lat + (BAND - 1) if up else lat - (BAND - 1)}
        return pltpu.make_async_remote_copy(
            src, fwd.at[at], send.at[item], f_in.at[at], device_id=where, device_id_type=MESH
        )

    def from_fwd(item, up):
        _, dst = ends(item, up)
        at = ROUTED.index(item)
        recv = up_recv if up else dn_recv
        where = {"lat": lat - (BAND - 2) if up else lat + (BAND - 2)}
        return pltpu.make_async_remote_copy(
            fwd.at[at], dst, f_out.at[at], recv.at[item], device_id=where, device_id_type=MESH
        )

    def start_lat(items, cond=True):
        for up, has, cross in ((True, has_up, cross_up), (False, has_dn, cross_dn)):
            plain = [item for item in items if item not in ROUTED]
            routed = [item for item in items if item in ROUTED]

            @pl.when(has & cond)
            def _():
                for item in plain:
                    to_lat(item, up).start()

            if routed:

                @pl.when(has & jnp.logical_not(cross) & cond)
                def _():
                    for item in routed:
                        to_lat(item, up).start()

                @pl.when(cross & cond)
                def _():
                    for item in routed:
                        to_fwd(item, up).start()

    def pass_on(items):
        for up, cond in ((True, fwd_up), (False, fwd_dn)):

            @pl.when(cond)
            def _():
                for item in items:
                    copy = from_fwd(item, up)
                    pltpu.make_async_remote_copy(
                        fwd.at[ROUTED.index(item)],
                        fwd.at[ROUTED.index(item)],
                        f_out.at[ROUTED.index(item)],
                        f_in.at[ROUTED.index(item)],
                        device_id={"lat": lat - 1 if up else lat + 1},
                        device_id_type=MESH,
                    ).wait_recv()
                    copy.start()

    def await_lat(items, cond=True):
        for up, has in ((True, has_dn), (False, has_up)):

            @pl.when(has & cond)
            def _():
                for item in items:
                    to_lat(item, up).wait_recv()

    def dual_to_prev(row):
        return pltpu.make_async_remote_copy(
            lam_send.at[row], l6.at[2 + row], tm_send.at[row], tm_recv.at[row],
            device_id={"tm": tm - 1}, device_id_type=MESH,
        )

    def prop_to_next(row):
        return pltpu.make_async_remote_copy(
            prop_send.at[row], arrived.at[row], tm_send.at[2 + row], tm_recv.at[2 + row],
            device_id={"tm": tm + 1}, device_id_type=MESH,
        )

    w3[1] = winds[...]
    for row in range(2):
        for at, size in CHUNKS:
            rows = pl.ds(at, size)
            dual = lam[row, rows, :]
            product_now = spread[row, rows, :] * dual
            lam_send[row, rows, :] = dual.astype(BF16)
            i6[2 + row, rows, :] = incr[row, rows, :].astype(BF16)
            scaled[row, rows, :] = product_now
            s6[2 + row, rows, :] = product_now.astype(BF16)

    @pl.when(jnp.logical_not(has_dn))
    def _():
        w3[0] = jnp.zeros_like(w3[0])
        for buffer in (i6, l6, s6):
            for row in (0, 1):
                buffer[row] = jnp.zeros_like(buffer[row])
        for m in range(NENS):
            q_recv[0, m] = jnp.zeros_like(q_recv[0, m])

    @pl.when(jnp.logical_not(has_up))
    def _():
        w3[2] = jnp.zeros_like(w3[2])
        for buffer in (i6, l6, s6):
            for row in (4, 5):
                buffer[row] = jnp.zeros_like(buffer[row])
        for m in range(NENS):
            q_recv[1, m] = jnp.zeros_like(q_recv[1, m])

    @pl.when(jnp.logical_not(has_prev))
    def _():
        arrived[...] = jnp.zeros_like(arrived)

    pl.semaphore_wait(barrier, targets)

    @pl.when(has_prev)
    def _():
        dual_to_prev(0).start()
        dual_to_prev(1).start()

    start_lat([WIN, INC, INC + 1], has_next)
    start_lat([SCA, SCA + 1])

    for base, matrix in ((0, mixing[...]), (4, vert[...])):
        mats[base], mats[base + 1] = split(matrix)
        mats[base + 2], mats[base + 3] = split(matrix.T)

    for at, size in CHUNKS:
        rows = pl.ds(at, size)
        totals = [None, None]
        duals = [lam[row, rows, :] for row in range(2)]
        for m in range(NENS):
            perturb = [members[row, m, rows, :].astype(F32) for row in range(2)]
            weighted = [perturb[row] * duals[row] for row in range(2)]
            for row in range(2):
                q_send[row, m, rows, :] = weighted[row].astype(BF16)
                near = weighted[1 - row] + east_of(weighted[row]) + west_of(weighted[row])
                term = perturb[row] * (weighted[row] + 0.25 * near)
                totals[row] = term if m == 0 else totals[row] + term
        for row in range(2):
            ens[row, rows, :] = totals[row]

    def weights(i):
        block, row = (i + 2) // 2, (i + 2) % 2
        north, south, east, west = (w3[block, 2 * p + row : 2 * p + row + 1, :] for p in range(4))
        return north, south, east, west, 1.0 - north - south - east - west

    low_edge = jnp.where(has_dn, 1.0, 0.0).astype(F32)
    high_edge = jnp.where(has_up, 1.0, 0.0).astype(F32)

    def inside(i, value):
        if i == -1:
            return value * low_edge
        if i == 2:
            return value * high_edge
        return value

    @pl.when(has_next)
    def _():
        await_lat([WIN, INC, INC + 1])

        def transport(of, i, rows):
            north, south, east, west, centre = weights(i)
            here = of(i, rows)
            total = centre * here + north * of(i + 1, rows) + south * of(i - 1, rows)
            return total + east * east_of(here) + west * west_of(here)

        def first(i, rows):
            if 0 <= i < 2:
                return incr[i, rows, :]
            return i6[i + 2, rows, :].astype(F32)

        for i in range(-1, 3):
            for at, size in CHUNKS:
                rows = pl.ds(at, size)
                za[i + 1, rows, :] = inside(i, transport(first, i, rows))
        for i in range(4):
            zb[i] = product(mats, 0, za[i])
        for i in range(2):
            for at, size in CHUNKS:
                rows = pl.ds(at, size)
                za[i, rows, :] = transport(lambda j, r: zb[j + 1, r, :], i, rows)
        for i in range(2):
            prop_send[i] = product(mats, 0, za[i]).astype(BF16)
            prop_to_next(i).start()

    for row in range(2):

        @pl.when(has_next)
        def _():
            dual_to_prev(row).wait_recv()

        start_lat([LNX + row], has_next)

    start_lat([QEN + m for m in range(NENS)])

    pass_on([SCA, SCA + 1])
    await_lat([SCA, SCA + 1])

    def smooth(of, i, rows):
        here = of(i, rows)
        return here + 0.25 * (of(i + 1, rows) + of(i - 1, rows) + east_of(here) + west_of(here))

    def field(i, rows):
        if 0 <= i < 2:
            return scaled[i, rows, :]
        return s6[i + 2, rows, :].astype(F32)

    for i in range(-1, 3):
        for at, size in CHUNKS:
            rows = pl.ds(at, size)
            za[i + 1, rows, :] = inside(i, smooth(field, i, rows))
    for i in range(2):
        for at, size in CHUNKS:
            rows = pl.ds(at, size)
            zb[i, rows, :] = smooth(lambda j, r: za[j + 1, r, :], i, rows)
    for i in range(2):
        za[i] = product(mats, 6, zb[i])
    for i in range(2):
        zb[i] = product(mats, 4, za[i])
    for i in range(2):
        for at, size in CHUNKS:
            rows = pl.ds(at, size)
            ens[i, rows, :] = (
                0.5 * (spread[i, rows, :] * zb[i, rows, :])
                + (0.5 / (NENS - 1)) * ens[i, rows, :]
                + incr[i, rows, :]
            )

    pass_on([QEN + 1, QEN + 2, QEN + 3])

    @pl.when(has_next)
    def _():
        await_lat([LNX, LNX + 1])

        def transport_back(of, i, rows):
            _, _, east, west, centre = weights(i)
            north, south = weights(i - 1)[0], weights(i + 1)[1]
            here = of(i, rows)
            total = centre * here + north * of(i - 1, rows) + south * of(i + 1, rows)
            return total + west_of(east * here) + east_of(west * here)

        for i in range(6):
            zb[i] = product_16(mats, 2, l6[i])
        for i in range(-1, 3):
            for at, size in CHUNKS:
                rows = pl.ds(at, size)
                za[i + 1, rows, :] = inside(
                    i, transport_back(lambda j, r: zb[j + 2, r, :], i, rows)
                )
        for i in range(4):
            zb[i] = product(mats, 2, za[i])
        for i in range(2):
            for at, size in CHUNKS:
                rows = pl.ds(at, size)
                back = transport_back(lambda j, r: zb[j + 1, r, :], i, rows)
                incr_out[i, rows, :] = lam[i, rows, :] - back

    @pl.when(jnp.logical_not(has_next))
    def _():
        incr_out[...] = lam[...]

    await_lat([QEN + m for m in range(NENS)])

    @pl.when(has_prev)
    def _():
        prop_from = [
            pltpu.make_async_remote_copy(
                prop_send.at[row], arrived.at[row], tm_send.at[2 + row], tm_recv.at[2 + row],
                device_id={"tm": tm - 1}, device_id_type=MESH,
            )
            for row in range(2)
        ]
        for copy in prop_from:
            copy.wait_recv()

    for i in range(2):
        for at, size in CHUNKS:
            rows = pl.ds(at, size)
            near = None
            for m in range(NENS):
                term = members[i, m, rows, :].astype(F32) * q_recv[i, m, rows, :].astype(F32)
                near = term if m == 0 else near + term
            lam_out[i, rows, :] = (
                ens[i, rows, :]
                + (0.5 * 0.25 / (NENS - 1)) * near
                - arrived[i, rows, :].astype(F32)
            )

    @pl.when(has_prev)
    def _():
        dual_to_prev(0).wait_send()
        dual_to_prev(1).wait_send()

    @pl.when(has_next)
    def _():
        prop_to_next(0).wait_send()
        prop_to_next(1).wait_send()

    for up, has in ((True, has_up), (False, has_dn)):

        @pl.when(has)
        def _():
            for item in [SCA, SCA + 1] + [QEN + m for m in range(NENS)]:
                to_lat(item, up).wait_send()

        @pl.when(has & has_next)
        def _():
            for item in [WIN, INC, INC + 1, LNX, LNX + 1]:
                to_lat(item, up).wait_send()

    for up, cond in ((True, fwd_up), (False, fwd_dn)):

        @pl.when(cond)
        def _():
            for item in ROUTED:
                from_fwd(item, up).wait_send()


def per_device(lam, incr, winds, mixing, spread, vert_corr, members):
    row = (COMP, LON)
    vmem = pl.BlockSpec(memory_space=pltpu.VMEM)
    state = jax.ShapeDtypeStruct((2, *row), F32)
    dma = pltpu.SemaphoreType.DMA
    scratch = [
        pltpu.VMEM((6, *row), BF16),
        pltpu.VMEM((6, *row), BF16),
        pltpu.VMEM((6, *row), BF16),
        pltpu.VMEM((3, 8, LON), F32),
        pltpu.VMEM((2, NENS, *row), BF16),
        pltpu.VMEM((2, NENS, *row), BF16),
        pltpu.VMEM((2, *row), BF16),
        pltpu.VMEM((2, *row), BF16),
        pltpu.VMEM((2, *row), BF16),
        pltpu.VMEM((len(ROUTED), *row), BF16),
        pltpu.VMEM((8, COMP, COMP), BF16),
        pltpu.VMEM((2, *row), F32),
        pltpu.VMEM((4, *row), F32),
        pltpu.VMEM((6, *row), F32),
        pltpu.VMEM((2, *row), F32),
        dma((4,)),
        dma((4,)),
        dma((ITEMS,)),
        dma((ITEMS,)),
        dma((ITEMS,)),
        dma((ITEMS,)),
        dma((len(ROUTED),)),
        dma((len(ROUTED),)),
    ]
    lam_result, incr_result = pl.pallas_call(
        kernel,
        out_shape=(state, state),
        in_specs=[vmem] * 7,
        out_specs=(vmem, vmem),
        scratch_shapes=scratch,
        compiler_params=pltpu.CompilerParams(
            collective_id=0, has_side_effects=True, vmem_limit_bytes=48 * 2**20
        ),
    )(
        lam[0],
        incr[0],
        winds[0].reshape(8, LON),
        mixing[0],
        spread[0],
        vert_corr,
        members[0],
    )
    return lam_result[None], incr_result[None]


def solution(mesh):
    in_specs = (
        P("tm", "lat", None, None),
        P("tm", "lat", None, None),
        P("tm", None, "lat", None),
        P("tm", None, None),
        P("tm", "lat", None, None),
        P(),
        P("tm", "lat", None, None, None),
    )
    out_specs = (P("tm", "lat", None, None), P("tm", "lat", None, None))
    return jax.shard_map(
        per_device, mesh=mesh, in_specs=in_specs, out_specs=out_specs, check_vma=False
    )
```

```python
import jax
import jax.numpy as jnp
from jax import lax
from jax.experimental import pallas as pl
from jax.experimental.pallas import tpu as pltpu
from jax.sharding import PartitionSpec as P

MESH = pl.DeviceIdType.MESH
F32, BF16 = jnp.float32, jnp.bfloat16
COMP, LON, NENS = 216, 256, 4
TM, LAT, BAND = 8, 64, 16
CHUNKS = [(at, min(32, COMP - at)) for at in range(0, COMP, 32)]

WIN, INC, SCA, LNX, QEN = 0, 1, 3, 5, 7
ITEMS = 11
PLACES = {"seven": 14, "six": 12, "one": 2}
ROUTES = {
    "seven": (SCA, SCA + 1, LNX + 1),
    "six": (QEN, QEN + 1),
    "one": (QEN + 2, QEN + 3),
}
ROUTED = {item: (kind, at) for kind, items in ROUTES.items() for at, item in enumerate(items)}


def split(value):
    high = value.astype(BF16)
    return high, (value - high.astype(F32)).astype(BF16)


def dot(a, b):
    return jnp.dot(a, b, preferred_element_type=F32)


def product(mats, base, value):
    high, low = split(value)
    return dot(mats[base], high) + (dot(mats[base + 1], high) + dot(mats[base], low))


def product_16(mats, base, value):
    return dot(mats[base], value) + dot(mats[base + 1], value)


def east_of(value):
    return pltpu.roll(value, LON - 1, 1)


def west_of(value):
    return pltpu.roll(value, 1, 1)


def kernel(
    lam_hbm, incr_hbm, winds_hbm, mixing_hbm, spread_hbm, vert_hbm, members_hbm, lam_out, incr_out,
    lam, incr, mixing, spread, vert, members,
    i6, l6, s6, w3, q_send, q_recv, lam_send, prop_send, arrived, fwd,
    mats, scaled, za, zb, ens,
    load_sem, tm_send, tm_recv, up_send, up_recv, dn_send, dn_recv, f_in, f_out,
):
    tm, lat = lax.axis_index("tm"), lax.axis_index("lat")
    place = lax.rem(lat, BAND)
    has_up, has_dn = lat < LAT - 1, lat > 0
    has_next, has_prev = tm < TM - 1, tm > 0
    cross_up = (place == BAND - 1) & has_up
    cross_dn = (place == 0) & has_dn

    def passes(kind, up):
        if up:
            return (place == PLACES[kind]) & (lat >= BAND)
        return (place == BAND - 1 - PLACES[kind]) & (lat < LAT - BAND)

    loads = [
        pltpu.make_async_copy(src, dst, load_sem.at[at])
        for at, (src, dst) in enumerate(
            (
                (lam_hbm, lam),
                (spread_hbm, spread),
                (incr_hbm, incr),
                (winds_hbm, w3.at[1]),
                (members_hbm, members),
                (mixing_hbm, mixing),
                (vert_hbm, vert),
            )
        )
    ]
    for load in loads:
        load.start()

    barrier = pltpu.get_barrier_semaphore()
    greetings = [
        (has_next, {"tm": tm + 1}),
        (has_prev, {"tm": tm - 1}),
        (has_up, {"lat": lat + 1}),
        (has_dn, {"lat": lat - 1}),
    ]
    for kind, p in PLACES.items():
        greetings += [
            (cross_up, {"lat": lat - p}),
            (cross_dn, {"lat": lat + p}),
            (passes(kind, True), {"lat": lat - p - 1}),
            (passes(kind, False), {"lat": lat + p + 1}),
        ]
    targets = 0
    for cond, where in greetings:
        targets = targets + jnp.where(cond, 1, 0)

        @pl.when(cond)
        def _():
            pl.semaphore_signal(barrier, inc=1, device_id=where, device_id_type=MESH)

    def ends(item, up):
        if item == WIN:
            return w3.at[1], w3.at[0 if up else 2]
        for first, buffer in ((INC, i6), (SCA, s6), (LNX, l6)):
            if first <= item < first + 2:
                row = item - first
                return buffer.at[2 + row], buffer.at[row if up else 4 + row]
        m = item - QEN
        return q_send.at[1 if up else 0, m], q_recv.at[0 if up else 1, m]

    def to_lat(item, up):
        src, dst = ends(item, up)
        send, recv = (up_send, up_recv) if up else (dn_send, dn_recv)
        where = {"lat": lat + 1 if up else lat - 1}
        return pltpu.make_async_remote_copy(
            src, dst, send.at[item], recv.at[item], device_id=where, device_id_type=MESH
        )

    def to_fwd(item, up):
        src, _ = ends(item, up)
        kind, at = ROUTED[item]
        send = up_send if up else dn_send
        p = PLACES[kind]
        where = {"lat": lat + p + 1 if up else lat - p - 1}
        return pltpu.make_async_remote_copy(
            src, fwd.at[at], send.at[item], f_in.at[at], device_id=where, device_id_type=MESH
        )

    def from_fwd(item, up):
        _, dst = ends(item, up)
        kind, at = ROUTED[item]
        recv = up_recv if up else dn_recv
        p = PLACES[kind]
        where = {"lat": lat - p if up else lat + p}
        return pltpu.make_async_remote_copy(
            fwd.at[at], dst, f_out.at[at], recv.at[item], device_id=where, device_id_type=MESH
        )

    def start_lat(items, cond=True, crossing=None):
        for up, has, cross in ((True, has_up, cross_up), (False, has_dn, cross_dn)):
            if crossing is not None:
                has = has & (cross if crossing else jnp.logical_not(cross))
            plain = [item for item in items if item not in ROUTED]
            routed = [item for item in items if item in ROUTED]

            @pl.when(has & cond)
            def _():
                for item in plain:
                    to_lat(item, up).start()

            if routed:

                @pl.when(has & jnp.logical_not(cross) & cond)
                def _():
                    for item in routed:
                        to_lat(item, up).start()

                @pl.when(has & cross & cond)
                def _():
                    for item in routed:
                        to_fwd(item, up).start()

    def pass_on(items, cond=True):
        for kind, routed in ROUTES.items():
            now = [item for item in items if item in routed]
            if not now:
                continue
            for up in (True, False):

                @pl.when(passes(kind, up) & cond)
                def _():
                    for item in now:
                        at = ROUTED[item][1]
                        pltpu.make_async_remote_copy(
                            fwd.at[at], fwd.at[at], f_out.at[at], f_in.at[at],
                            device_id={"lat": lat - 1 if up else lat + 1}, device_id_type=MESH,
                        ).wait_recv()
                        from_fwd(item, up).start()

    def await_lat(items, cond=True):
        for up, has in ((True, has_dn), (False, has_up)):

            @pl.when(has & cond)
            def _():
                for item in items:
                    to_lat(item, up).wait_recv()

    def dual_to_prev(row):
        return pltpu.make_async_remote_copy(
            lam_send.at[row], l6.at[2 + row], tm_send.at[row], tm_recv.at[row],
            device_id={"tm": tm - 1}, device_id_type=MESH,
        )

    def prop_to_next(row):
        return pltpu.make_async_remote_copy(
            prop_send.at[row], arrived.at[row], tm_send.at[2 + row], tm_recv.at[2 + row],
            device_id={"tm": tm + 1}, device_id_type=MESH,
        )

    for load in loads[:4]:
        load.wait()
    for row in range(2):
        for at, size in CHUNKS:
            rows = pl.ds(at, size)
            dual = lam[row, rows, :]
            product_now = spread[row, rows, :] * dual
            lam_send[row, rows, :] = dual.astype(BF16)
            i6[2 + row, rows, :] = incr[row, rows, :].astype(BF16)
            scaled[row, rows, :] = product_now
            s6[2 + row, rows, :] = product_now.astype(BF16)

    @pl.when(jnp.logical_not(has_dn))
    def _():
        w3[0] = jnp.zeros_like(w3[0])
        for buffer in (i6, l6, s6):
            for row in (0, 1):
                buffer[row] = jnp.zeros_like(buffer[row])
        for m in range(NENS):
            q_recv[0, m] = jnp.zeros_like(q_recv[0, m])

    @pl.when(jnp.logical_not(has_up))
    def _():
        w3[2] = jnp.zeros_like(w3[2])
        for buffer in (i6, l6, s6):
            for row in (4, 5):
                buffer[row] = jnp.zeros_like(buffer[row])
        for m in range(NENS):
            q_recv[1, m] = jnp.zeros_like(q_recv[1, m])

    @pl.when(jnp.logical_not(has_prev))
    def _():
        arrived[...] = jnp.zeros_like(arrived)

    pl.semaphore_wait(barrier, targets)

    @pl.when(has_prev)
    def _():
        dual_to_prev(0).start()
        dual_to_prev(1).start()

    start_lat([WIN, INC, INC + 1], has_next)
    start_lat([SCA, SCA + 1])

    for load in loads[4:]:
        load.wait()
    for base, matrix in ((0, mixing[...]), (4, vert[...])):
        mats[base], mats[base + 1] = split(matrix)
        mats[base + 2], mats[base + 3] = split(matrix.T)

    for at, size in CHUNKS:
        rows = pl.ds(at, size)
        totals = [None, None]
        duals = [lam[row, rows, :] for row in range(2)]
        for m in range(NENS):
            perturb = [members[row, m, rows, :].astype(F32) for row in range(2)]
            weighted = [perturb[row] * duals[row] for row in range(2)]
            for row in range(2):
                q_send[row, m, rows, :] = weighted[row].astype(BF16)
                near = weighted[1 - row] + east_of(weighted[row]) + west_of(weighted[row])
                term = perturb[row] * (weighted[row] + 0.25 * near)
                totals[row] = term if m == 0 else totals[row] + term
        for row in range(2):
            ens[row, rows, :] = totals[row]

    edges = [QEN + m for m in range(NENS)]
    start_lat(edges, crossing=True)

    def weights(i):
        block, row = (i + 2) // 2, (i + 2) % 2
        north, south, east, west = (w3[block, p, row : row + 1, :] for p in range(4))
        return north, south, east, west, 1.0 - north - south - east - west

    low_edge = jnp.where(has_dn, 1.0, 0.0).astype(F32)
    high_edge = jnp.where(has_up, 1.0, 0.0).astype(F32)

    def inside(i, value):
        if i == -1:
            return value * low_edge
        if i == 2:
            return value * high_edge
        return value

    @pl.when(has_next)
    def _():
        await_lat([WIN, INC, INC + 1])

        def transport(of, i, rows):
            north, south, east, west, centre = weights(i)
            here = of(i, rows)
            total = centre * here + north * of(i + 1, rows) + south * of(i - 1, rows)
            return total + east * east_of(here) + west * west_of(here)

        def first(i, rows):
            if 0 <= i < 2:
                return incr[i, rows, :]
            return i6[i + 2, rows, :].astype(F32)

        for i in range(-1, 3):
            for at, size in CHUNKS:
                rows = pl.ds(at, size)
                za[i + 1, rows, :] = inside(i, transport(first, i, rows))
        for i in range(4):
            zb[i] = product(mats, 0, za[i])
        for i in range(2):
            for at, size in CHUNKS:
                rows = pl.ds(at, size)
                za[i, rows, :] = transport(lambda j, r: zb[j + 1, r, :], i, rows)
        for i in range(2):
            prop_send[i] = product(mats, 0, za[i]).astype(BF16)
            prop_to_next(i).start()

    pass_on([SCA, SCA + 1])

    for row in range(2):

        @pl.when(has_next)
        def _():
            dual_to_prev(row).wait_recv()

        start_lat([LNX + row], has_next)

    start_lat(edges, crossing=False)

    pass_on(edges)
    pass_on([LNX + 1], has_next)
    await_lat([SCA, SCA + 1])

    def smooth(of, i, rows):
        here = of(i, rows)
        return here + 0.25 * (of(i + 1, rows) + of(i - 1, rows) + east_of(here) + west_of(here))

    def field(i, rows):
        if 0 <= i < 2:
            return scaled[i, rows, :]
        return s6[i + 2, rows, :].astype(F32)

    for i in range(-1, 3):
        for at, size in CHUNKS:
            rows = pl.ds(at, size)
            za[i + 1, rows, :] = inside(i, smooth(field, i, rows))
    for i in range(2):
        for at, size in CHUNKS:
            rows = pl.ds(at, size)
            zb[i, rows, :] = smooth(lambda j, r: za[j + 1, r, :], i, rows)
    for i in range(2):
        za[i] = product(mats, 6, zb[i])
    for i in range(2):
        zb[i] = product(mats, 4, za[i])
    for i in range(2):
        for at, size in CHUNKS:
            rows = pl.ds(at, size)
            ens[i, rows, :] = (
                0.5 * (spread[i, rows, :] * zb[i, rows, :])
                + (0.5 / (NENS - 1)) * ens[i, rows, :]
                + incr[i, rows, :]
            )

    @pl.when(has_next)
    def _():
        await_lat([LNX, LNX + 1])

        def transport_back(of, i, rows):
            _, _, east, west, centre = weights(i)
            north, south = weights(i - 1)[0], weights(i + 1)[1]
            here = of(i, rows)
            total = centre * here + north * of(i - 1, rows) + south * of(i + 1, rows)
            return total + west_of(east * here) + east_of(west * here)

        for i in range(6):
            zb[i] = product_16(mats, 2, l6[i])
        for i in range(-1, 3):
            for at, size in CHUNKS:
                rows = pl.ds(at, size)
                za[i + 1, rows, :] = inside(
                    i, transport_back(lambda j, r: zb[j + 2, r, :], i, rows)
                )
        for i in range(4):
            zb[i] = product(mats, 2, za[i])
        for i in range(2):
            for at, size in CHUNKS:
                rows = pl.ds(at, size)
                back = transport_back(lambda j, r: zb[j + 1, r, :], i, rows)
                incr_out[i, rows, :] = lam[i, rows, :] - back

    @pl.when(jnp.logical_not(has_next))
    def _():
        incr_out[...] = lam[...]

    await_lat(edges)

    @pl.when(has_prev)
    def _():
        prop_from = [
            pltpu.make_async_remote_copy(
                prop_send.at[row], arrived.at[row], tm_send.at[2 + row], tm_recv.at[2 + row],
                device_id={"tm": tm - 1}, device_id_type=MESH,
            )
            for row in range(2)
        ]
        for copy in prop_from:
            copy.wait_recv()

    for i in range(2):
        for at, size in CHUNKS:
            rows = pl.ds(at, size)
            near = None
            for m in range(NENS):
                term = members[i, m, rows, :].astype(F32) * q_recv[i, m, rows, :].astype(F32)
                near = term if m == 0 else near + term
            lam_out[i, rows, :] = (
                ens[i, rows, :]
                + (0.5 * 0.25 / (NENS - 1)) * near
                - arrived[i, rows, :].astype(F32)
            )

    @pl.when(has_prev)
    def _():
        dual_to_prev(0).wait_send()
        dual_to_prev(1).wait_send()

    @pl.when(has_next)
    def _():
        prop_to_next(0).wait_send()
        prop_to_next(1).wait_send()

    for up, has in ((True, has_up), (False, has_dn)):

        @pl.when(has)
        def _():
            for item in [SCA, SCA + 1, *edges]:
                to_lat(item, up).wait_send()

        @pl.when(has & has_next)
        def _():
            for item in [WIN, INC, INC + 1, LNX, LNX + 1]:
                to_lat(item, up).wait_send()

    for kind, routed in ROUTES.items():
        for up in (True, False):
            for item in routed:

                @pl.when(passes(kind, up) & (has_next if item in (LNX, LNX + 1) else True))
                def _():
                    from_fwd(item, up).wait_send()


def per_device(lam, incr, winds, mixing, spread, vert_corr, members):
    row = (COMP, LON)
    vmem = pl.BlockSpec(memory_space=pltpu.VMEM)
    state = jax.ShapeDtypeStruct((2, *row), F32)
    dma = pltpu.SemaphoreType.DMA
    scratch = [
        pltpu.VMEM((2, *row), F32),
        pltpu.VMEM((2, *row), F32),
        pltpu.VMEM((COMP, COMP), F32),
        pltpu.VMEM((2, *row), F32),
        pltpu.VMEM((COMP, COMP), F32),
        pltpu.VMEM((2, NENS, *row), BF16),
        pltpu.VMEM((6, *row), BF16),
        pltpu.VMEM((6, *row), BF16),
        pltpu.VMEM((6, *row), BF16),
        pltpu.VMEM((3, 4, 2, LON), F32),
        pltpu.VMEM((2, NENS, *row), BF16),
        pltpu.VMEM((2, NENS, *row), BF16),
        pltpu.VMEM((2, *row), BF16),
        pltpu.VMEM((2, *row), BF16),
        pltpu.VMEM((2, *row), BF16),
        pltpu.VMEM((3, *row), BF16),
        pltpu.VMEM((8, COMP, COMP), BF16),
        pltpu.VMEM((2, *row), F32),
        pltpu.VMEM((4, *row), F32),
        pltpu.VMEM((6, *row), F32),
        pltpu.VMEM((2, *row), F32),
        dma((7,)),
        dma((4,)),
        dma((4,)),
        dma((ITEMS,)),
        dma((ITEMS,)),
        dma((ITEMS,)),
        dma((ITEMS,)),
        dma((3,)),
        dma((3,)),
    ]
    lam_result, incr_result = pl.pallas_call(
        kernel,
        out_shape=(state, state),
        in_specs=[pl.BlockSpec(memory_space=pltpu.HBM)] * 7,
        out_specs=(vmem, vmem),
        scratch_shapes=scratch,
        compiler_params=pltpu.CompilerParams(
            collective_id=0, has_side_effects=True, vmem_limit_bytes=60 * 2**20
        ),
    )(
        lam[0],
        incr[0],
        winds[0],
        mixing[0],
        spread[0],
        vert_corr,
        members[0],
    )
    return lam_result[None], incr_result[None]


def solution(mesh):
    in_specs = (
        P("tm", "lat", None, None),
        P("tm", "lat", None, None),
        P("tm", None, "lat", None),
        P("tm", None, None),
        P("tm", "lat", None, None),
        P(),
        P("tm", "lat", None, None, None),
    )
    out_specs = (P("tm", "lat", None, None), P("tm", "lat", None, None))
    return jax.shard_map(
        per_device, mesh=mesh, in_specs=in_specs, out_specs=out_specs, check_vma=False
    )
```

```python
import jax
import jax.numpy as jnp
from jax import lax
from jax.experimental import pallas as pl
from jax.experimental.pallas import tpu as pltpu
from jax.sharding import PartitionSpec as P

MESH = pl.DeviceIdType.MESH
F32, BF16 = jnp.float32, jnp.bfloat16
COMP, LON, NENS = 216, 256, 4
TM, LAT, BAND = 8, 64, 16
CHUNKS = [(at, min(32, COMP - at)) for at in range(0, COMP, 32)]

WIN, INC, SCA, LNX, QEN = 0, 1, 3, 5, 7
ITEMS = 11
PLACES = {"seven": 14, "six": 12, "one": 2}
ROUTES = {
    "seven": (INC, INC + 1, QEN, QEN + 1),
    "six": (SCA, SCA + 1, QEN + 2, QEN + 3),
    "one": (SCA, SCA + 1, QEN + 2, QEN + 3),
}
KINDS = {True: ("seven", "six"), False: ("one",)}
FAR = len(ROUTES["seven"])
SLOTS = FAR + 2


def route(item, even):
    for kind in KINDS[even]:
        if item in ROUTES[kind]:
            return kind, ROUTES[kind].index(item)
    return None


def split(value):
    high = value.astype(BF16)
    return high, (value - high.astype(F32)).astype(BF16)


def dot(a, b):
    return jnp.dot(a, b, preferred_element_type=F32)


def product(mats, base, value):
    high, low = split(value)
    return dot(mats[base], high) + (dot(mats[base + 1], high) + dot(mats[base], low))


def product_16(mats, base, value):
    return dot(mats[base], value) + dot(mats[base + 1], value)


def east_of(value):
    return pltpu.roll(value, LON - 1, 1)


def west_of(value):
    return pltpu.roll(value, 1, 1)


def kernel(
    lam_hbm, incr_hbm, winds_hbm, mixing_hbm, spread_hbm, vert_hbm, members_hbm, lam_out, incr_out,
    lam, incr, mixing, spread, vert, members,
    i6, l6, s6, w3, q_send, q_recv, lam_send, prop_send, arrived, fwd,
    mats, scaled, za, zb, ens,
    load_sem, tm_send, tm_recv, up_send, up_recv, dn_send, dn_recv, f_in, f_out, far_send,
):
    tm, lat = lax.axis_index("tm"), lax.axis_index("lat")
    place = lax.rem(lat, BAND)
    has_up, has_dn = lat < LAT - 1, lat > 0
    has_next, has_prev = tm < TM - 1, tm > 0
    cross_up = (place == BAND - 1) & has_up
    cross_dn = (place == 0) & has_dn

    is_even = lax.rem(tm, 2) == 0
    is_odd = jnp.logical_not(is_even)

    def at_place(kind, up):
        if up:
            return (place == PLACES[kind]) & (lat >= BAND)
        return (place == BAND - 1 - PLACES[kind]) & (lat < LAT - BAND)

    def of_tm(kind):
        return is_even if kind in KINDS[True] else is_odd

    def passes(kind, up):
        return at_place(kind, up) & of_tm(kind)

    def straight(up):
        return is_even if up else is_odd

    def passes_dual(up):
        return at_place("seven", up) & straight(up) & has_next

    def sends_dual(up):
        return (cross_up if up else cross_dn) & jnp.logical_not(straight(up)) & has_prev

    loads = [
        pltpu.make_async_copy(src, dst, load_sem.at[at])
        for at, (src, dst) in enumerate(
            (
                (lam_hbm, lam),
                (spread_hbm, spread),
                (incr_hbm, incr),
                (winds_hbm, w3.at[1]),
                (members_hbm, members),
                (mixing_hbm, mixing),
                (vert_hbm, vert),
            )
        )
    ]
    for load in loads:
        load.start()

    barrier = pltpu.get_barrier_semaphore()
    greetings = [
        (has_next, {"tm": tm + 1}, has_prev),
        (has_prev, {"tm": tm - 1}, has_next),
        (has_up, {"lat": lat + 1}, has_dn),
        (has_dn, {"lat": lat - 1}, has_up),
        (cross_up & is_odd & has_next, {"lat": lat - PLACES["seven"]}, passes_dual(False)),
        (passes_dual(True), {"tm": tm + 1, "lat": lat - PLACES["seven"] - 1}, sends_dual(True)),
        (passes_dual(False), {"tm": tm + 1, "lat": lat + PLACES["seven"] + 1}, sends_dual(False)),
        (cross_up & is_even & has_next, {"tm": tm + 1, "lat": lat + 1}, cross_dn & is_odd & has_prev),
    ]
    for kind, p in PLACES.items():
        greetings += [
            (cross_up & of_tm(kind), {"lat": lat - p}, passes(kind, False)),
            (cross_dn & of_tm(kind), {"lat": lat + p}, passes(kind, True)),
            (passes(kind, True), {"lat": lat - p - 1}, cross_up & of_tm(kind)),
            (passes(kind, False), {"lat": lat + p + 1}, cross_dn & of_tm(kind)),
        ]
    targets = 0
    for cond, where, mirrored in greetings:
        targets = targets + jnp.where(mirrored, 1, 0)

        @pl.when(cond)
        def _():
            pl.semaphore_signal(barrier, inc=1, device_id=where, device_id_type=MESH)

    def ends(item, up):
        if item == WIN:
            return w3.at[1], w3.at[0 if up else 2]
        for first, buffer in ((INC, i6), (SCA, s6), (LNX, l6)):
            if first <= item < first + 2:
                row = item - first
                return buffer.at[2 + row], buffer.at[row if up else 4 + row]
        m = item - QEN
        return q_send.at[1 if up else 0, m], q_recv.at[0 if up else 1, m]

    def to_lat(item, up):
        src, dst = ends(item, up)
        send, recv = (up_send, up_recv) if up else (dn_send, dn_recv)
        where = {"lat": lat + 1 if up else lat - 1}
        return pltpu.make_async_remote_copy(
            src, dst, send.at[item], recv.at[item], device_id=where, device_id_type=MESH
        )

    def dual_across(row, up):
        where = {"tm": tm - 1, "lat": lat + BAND - 1 if up else lat - BAND + 1}
        return pltpu.make_async_remote_copy(
            lam_send.at[row], fwd.at[FAR + row], far_send.at[row], f_in.at[FAR + row],
            device_id=where, device_id_type=MESH,
        )

    def dual_direct(row):
        return pltpu.make_async_remote_copy(
            lam_send.at[row], l6.at[4 + row], far_send.at[row], dn_recv.at[LNX + row],
            device_id={"tm": tm - 1, "lat": lat - 1}, device_id_type=MESH,
        )

    def to_fwd(item, up, even):
        src, _ = ends(item, up)
        kind, at = route(item, even)
        send = up_send if up else dn_send
        p = PLACES[kind]
        where = {"lat": lat + p + 1 if up else lat - p - 1}
        return pltpu.make_async_remote_copy(
            src, fwd.at[at], send.at[item], f_in.at[at], device_id=where, device_id_type=MESH
        )

    def from_fwd(item, kind, at, up):
        _, dst = ends(item, up)
        recv = up_recv if up else dn_recv
        p = PLACES[kind]
        where = {"lat": lat - p if up else lat + p}
        return pltpu.make_async_remote_copy(
            fwd.at[at], dst, f_out.at[at], recv.at[item], device_id=where, device_id_type=MESH
        )

    def start_lat(items, cond=True, sides=(True, False)):
        for up, has, cross in ((True, has_up, cross_up), (False, has_dn, cross_dn)):
            if False in sides:

                @pl.when(has & jnp.logical_not(cross) & cond)
                def _():
                    for item in items:
                        to_lat(item, up).start()

            if True not in sides:
                continue
            for even in (True, False):

                @pl.when(cross & (is_even if even else is_odd) & cond)
                def _():
                    for item in items:
                        if route(item, even):
                            to_fwd(item, up, even).start()
                        elif item not in (LNX, LNX + 1) or (up and not even):
                            to_lat(item, up).start()

    def hand_over(item, kind, at, up):
        pltpu.make_async_remote_copy(
            fwd.at[at], fwd.at[at], f_out.at[at], f_in.at[at],
            device_id={"lat": lat - 1 if up else lat + 1}, device_id_type=MESH,
        ).wait_recv()
        from_fwd(item, kind, at, up).start()

    def pass_on(items, cond=True):
        for kind, routed in ROUTES.items():
            now = [item for item in items if item in routed]
            if not now:
                continue
            for up in (True, False):

                @pl.when(passes(kind, up) & cond)
                def _():
                    for item in now:
                        hand_over(item, kind, routed.index(item), up)

    def pass_duals():
        for up in (True, False):

            @pl.when(passes_dual(up))
            def _():
                for row in range(2):
                    hand_over(LNX + row, "seven", FAR + row, up)

    def await_lat(items, cond=True):
        for up, has in ((True, has_dn), (False, has_up)):

            @pl.when(has & cond)
            def _():
                for item in items:
                    to_lat(item, up).wait_recv()

    def dual_to_prev(row):
        return pltpu.make_async_remote_copy(
            lam_send.at[row], l6.at[2 + row], tm_send.at[row], tm_recv.at[row],
            device_id={"tm": tm - 1}, device_id_type=MESH,
        )

    def prop_to_next(row):
        return pltpu.make_async_remote_copy(
            prop_send.at[row], arrived.at[row], tm_send.at[2 + row], tm_recv.at[2 + row],
            device_id={"tm": tm + 1}, device_id_type=MESH,
        )

    for load in loads[:4]:
        load.wait()
    for row in range(2):
        for at, size in CHUNKS:
            rows = pl.ds(at, size)
            dual = lam[row, rows, :]
            product_now = spread[row, rows, :] * dual
            lam_send[row, rows, :] = dual.astype(BF16)
            i6[2 + row, rows, :] = incr[row, rows, :].astype(BF16)
            scaled[row, rows, :] = product_now
            s6[2 + row, rows, :] = product_now.astype(BF16)

    @pl.when(jnp.logical_not(has_dn))
    def _():
        w3[0] = jnp.zeros_like(w3[0])
        for buffer in (i6, l6, s6):
            for row in (0, 1):
                buffer[row] = jnp.zeros_like(buffer[row])
        for m in range(NENS):
            q_recv[0, m] = jnp.zeros_like(q_recv[0, m])

    @pl.when(jnp.logical_not(has_up))
    def _():
        w3[2] = jnp.zeros_like(w3[2])
        for buffer in (i6, l6, s6):
            for row in (4, 5):
                buffer[row] = jnp.zeros_like(buffer[row])
        for m in range(NENS):
            q_recv[1, m] = jnp.zeros_like(q_recv[1, m])

    @pl.when(jnp.logical_not(has_prev))
    def _():
        arrived[...] = jnp.zeros_like(arrived)

    pl.semaphore_wait(barrier, targets)

    @pl.when(has_prev)
    def _():
        dual_to_prev(0).start()
        dual_to_prev(1).start()

    start_lat([WIN, INC, INC + 1], has_next)
    start_lat([SCA, SCA + 1])
    for up in (True, False):

        @pl.when(sends_dual(up))
        def _():
            for row in range(2):
                dual_across(row, up).start()

    @pl.when(cross_dn & is_odd & has_prev)
    def _():
        for row in range(2):
            dual_direct(row).start()

    for load in loads[4:]:
        load.wait()
    for base, matrix in ((0, mixing[...]), (4, vert[...])):
        mats[base], mats[base + 1] = split(matrix)
        mats[base + 2], mats[base + 3] = split(matrix.T)

    for at, size in CHUNKS:
        rows = pl.ds(at, size)
        totals = [None, None]
        duals = [lam[row, rows, :] for row in range(2)]
        for m in range(NENS):
            perturb = [members[row, m, rows, :].astype(F32) for row in range(2)]
            weighted = [perturb[row] * duals[row] for row in range(2)]
            for row in range(2):
                q_send[row, m, rows, :] = weighted[row].astype(BF16)
                near = weighted[1 - row] + east_of(weighted[row]) + west_of(weighted[row])
                term = perturb[row] * (weighted[row] + 0.25 * near)
                totals[row] = term if m == 0 else totals[row] + term
        for row in range(2):
            ens[row, rows, :] = totals[row]

    edges = [QEN + m for m in range(NENS)]
    start_lat(edges, sides=(True,))
    pass_on([INC, INC + 1], has_next)

    def weights(i):
        block, row = (i + 2) // 2, (i + 2) % 2
        north, south, east, west = (w3[block, p, row : row + 1, :] for p in range(4))
        return north, south, east, west, 1.0 - north - south - east - west

    low_edge = jnp.where(has_dn, 1.0, 0.0).astype(F32)
    high_edge = jnp.where(has_up, 1.0, 0.0).astype(F32)

    def inside(i, value):
        if i == -1:
            return value * low_edge
        if i == 2:
            return value * high_edge
        return value

    @pl.when(has_next)
    def _():
        await_lat([WIN, INC, INC + 1])

        def transport(of, i, rows):
            north, south, east, west, centre = weights(i)
            here = of(i, rows)
            total = centre * here + north * of(i + 1, rows) + south * of(i - 1, rows)
            return total + east * east_of(here) + west * west_of(here)

        def first(i, rows):
            if 0 <= i < 2:
                return incr[i, rows, :]
            return i6[i + 2, rows, :].astype(F32)

        for i in range(-1, 3):
            for at, size in CHUNKS:
                rows = pl.ds(at, size)
                za[i + 1, rows, :] = inside(i, transport(first, i, rows))
        for i in range(4):
            zb[i] = product(mats, 0, za[i])
        for i in range(2):
            for at, size in CHUNKS:
                rows = pl.ds(at, size)
                za[i, rows, :] = transport(lambda j, r: zb[j + 1, r, :], i, rows)
        for i in range(2):
            prop_send[i] = product(mats, 0, za[i]).astype(BF16)
            prop_to_next(i).start()

    pass_on([SCA, SCA + 1])
    pass_duals()

    for row in range(2):

        @pl.when(has_next)
        def _():
            dual_to_prev(row).wait_recv()

        start_lat([LNX + row], has_next)

    start_lat(edges, sides=(False,))
    pass_on(edges)

    await_lat([SCA, SCA + 1])

    def smooth(of, i, rows):
        here = of(i, rows)
        return here + 0.25 * (of(i + 1, rows) + of(i - 1, rows) + east_of(here) + west_of(here))

    def field(i, rows):
        if 0 <= i < 2:
            return scaled[i, rows, :]
        return s6[i + 2, rows, :].astype(F32)

    for i in range(-1, 3):
        for at, size in CHUNKS:
            rows = pl.ds(at, size)
            za[i + 1, rows, :] = inside(i, smooth(field, i, rows))
    for i in range(2):
        for at, size in CHUNKS:
            rows = pl.ds(at, size)
            zb[i, rows, :] = smooth(lambda j, r: za[j + 1, r, :], i, rows)
    for i in range(2):
        za[i] = product(mats, 6, zb[i])
    for i in range(2):
        zb[i] = product(mats, 4, za[i])
    for i in range(2):
        for at, size in CHUNKS:
            rows = pl.ds(at, size)
            ens[i, rows, :] = (
                0.5 * (spread[i, rows, :] * zb[i, rows, :])
                + (0.5 / (NENS - 1)) * ens[i, rows, :]
                + incr[i, rows, :]
            )

    @pl.when(has_next)
    def _():
        await_lat([LNX, LNX + 1])

        def transport_back(of, i, rows):
            _, _, east, west, centre = weights(i)
            north, south = weights(i - 1)[0], weights(i + 1)[1]
            here = of(i, rows)
            total = centre * here + north * of(i - 1, rows) + south * of(i + 1, rows)
            return total + west_of(east * here) + east_of(west * here)

        for i in range(6):
            zb[i] = product_16(mats, 2, l6[i])
        for i in range(-1, 3):
            for at, size in CHUNKS:
                rows = pl.ds(at, size)
                za[i + 1, rows, :] = inside(
                    i, transport_back(lambda j, r: zb[j + 2, r, :], i, rows)
                )
        for i in range(4):
            zb[i] = product(mats, 2, za[i])
        for i in range(2):
            for at, size in CHUNKS:
                rows = pl.ds(at, size)
                back = transport_back(lambda j, r: zb[j + 1, r, :], i, rows)
                incr_out[i, rows, :] = lam[i, rows, :] - back

    @pl.when(jnp.logical_not(has_next))
    def _():
        incr_out[...] = lam[...]

    await_lat(edges)

    @pl.when(has_prev)
    def _():
        prop_from = [
            pltpu.make_async_remote_copy(
                prop_send.at[row], arrived.at[row], tm_send.at[2 + row], tm_recv.at[2 + row],
                device_id={"tm": tm - 1}, device_id_type=MESH,
            )
            for row in range(2)
        ]
        for copy in prop_from:
            copy.wait_recv()

    for i in range(2):
        for at, size in CHUNKS:
            rows = pl.ds(at, size)
            near = None
            for m in range(NENS):
                term = members[i, m, rows, :].astype(F32) * q_recv[i, m, rows, :].astype(F32)
                near = term if m == 0 else near + term
            lam_out[i, rows, :] = (
                ens[i, rows, :]
                + (0.5 * 0.25 / (NENS - 1)) * near
                - arrived[i, rows, :].astype(F32)
            )

    @pl.when(has_prev)
    def _():
        dual_to_prev(0).wait_send()
        dual_to_prev(1).wait_send()

    @pl.when(has_next)
    def _():
        prop_to_next(0).wait_send()
        prop_to_next(1).wait_send()

    @pl.when(cross_dn & is_odd & has_prev)
    def _():
        for row in range(2):
            dual_direct(row).wait_send()

    for up, has, cross in ((True, has_up, cross_up), (False, has_dn, cross_dn)):

        @pl.when(has)
        def _():
            for item in [SCA, SCA + 1, *edges]:
                to_lat(item, up).wait_send()

        @pl.when(has & has_next)
        def _():
            for item in [WIN, INC, INC + 1]:
                to_lat(item, up).wait_send()

        @pl.when(has & has_next & (jnp.logical_not(cross) | (is_odd if up else False)))
        def _():
            for item in [LNX, LNX + 1]:
                to_lat(item, up).wait_send()

        @pl.when(sends_dual(up))
        def _():
            for row in range(2):
                dual_across(row, up).wait_send()

        for kind, routed in ROUTES.items():
            for at, item in enumerate(routed):

                @pl.when(passes(kind, up) & (has_next if item in (INC, INC + 1) else True))
                def _():
                    from_fwd(item, kind, at, up).wait_send()

        @pl.when(passes_dual(up))
        def _():
            for row in range(2):
                from_fwd(LNX + row, "seven", FAR + row, up).wait_send()


def per_device(lam, incr, winds, mixing, spread, vert_corr, members):
    row = (COMP, LON)
    vmem = pl.BlockSpec(memory_space=pltpu.VMEM)
    state = jax.ShapeDtypeStruct((2, *row), F32)
    dma = pltpu.SemaphoreType.DMA
    scratch = [
        pltpu.VMEM((2, *row), F32),
        pltpu.VMEM((2, *row), F32),
        pltpu.VMEM((COMP, COMP), F32),
        pltpu.VMEM((2, *row), F32),
        pltpu.VMEM((COMP, COMP), F32),
        pltpu.VMEM((2, NENS, *row), BF16),
        pltpu.VMEM((6, *row), BF16),
        pltpu.VMEM((6, *row), BF16),
        pltpu.VMEM((6, *row), BF16),
        pltpu.VMEM((3, 4, 2, LON), F32),
        pltpu.VMEM((2, NENS, *row), BF16),
        pltpu.VMEM((2, NENS, *row), BF16),
        pltpu.VMEM((2, *row), BF16),
        pltpu.VMEM((2, *row), BF16),
        pltpu.VMEM((2, *row), BF16),
        pltpu.VMEM((SLOTS, *row), BF16),
        pltpu.VMEM((8, COMP, COMP), BF16),
        pltpu.VMEM((2, *row), F32),
        pltpu.VMEM((4, *row), F32),
        pltpu.VMEM((6, *row), F32),
        pltpu.VMEM((2, *row), F32),
        dma((7,)),
        dma((4,)),
        dma((4,)),
        dma((ITEMS,)),
        dma((ITEMS,)),
        dma((ITEMS,)),
        dma((ITEMS,)),
        dma((SLOTS,)),
        dma((SLOTS,)),
        dma((2,)),
    ]
    lam_result, incr_result = pl.pallas_call(
        kernel,
        out_shape=(state, state),
        in_specs=[pl.BlockSpec(memory_space=pltpu.HBM)] * 7,
        out_specs=(vmem, vmem),
        scratch_shapes=scratch,
        compiler_params=pltpu.CompilerParams(
            collective_id=0, has_side_effects=True, vmem_limit_bytes=48 * 2**20
        ),
    )(
        *(
            pltpu.with_memory_space_constraint(array, pltpu.HBM)
            for array in (lam[0], incr[0], winds[0], mixing[0], spread[0], vert_corr, members[0])
        )
    )
    return lam_result[None], incr_result[None]


def solution(mesh):
    in_specs = (
        P("tm", "lat", None, None),
        P("tm", "lat", None, None),
        P("tm", None, "lat", None),
        P("tm", None, None),
        P("tm", "lat", None, None),
        P(),
        P("tm", "lat", None, None, None),
    )
    out_specs = (P("tm", "lat", None, None), P("tm", "lat", None, None))
    return jax.shard_map(
        per_device, mesh=mesh, in_specs=in_specs, out_specs=out_specs, check_vma=False
    )
```

```python
import jax
import jax.numpy as jnp
from jax import lax
from jax.experimental import pallas as pl
from jax.experimental.pallas import tpu as pltpu
from jax.sharding import PartitionSpec as P

MESH = pl.DeviceIdType.MESH
F32, BF16 = jnp.float32, jnp.bfloat16
COMP, LON, NENS = 216, 256, 4
TM, LAT, BAND = 8, 64, 16
CHUNKS = [(at, min(32, COMP - at)) for at in range(0, COMP, 32)]

WIN, INC, SCA, LNX, QEN = 0, 1, 3, 5, 7
ITEMS = 11
PLACES = {"seven": 14, "six": 12, "one": 2}
ROUTES = {
    True: {"seven": (SCA, SCA + 1, QEN), "six": (QEN + 2, QEN + 3)},
    False: {"seven": (QEN, QEN + 1), "one": (SCA, SCA + 1, QEN + 2, QEN + 3)},
}
RELAYS = [(kind, even) for even, kinds in ROUTES.items() for kind in kinds]
FAR = 4
SLOTS = FAR + 2


def route(item, even):
    for kind, items in ROUTES[even].items():
        if item in items:
            return kind, items.index(item)
    return None


def split(value):
    high = value.astype(BF16)
    return high, (value - high.astype(F32)).astype(BF16)


def dot(a, b):
    return jnp.dot(a, b, preferred_element_type=F32)


def product(mats, base, value):
    high, low = split(value)
    return dot(mats[base], high) + (dot(mats[base + 1], high) + dot(mats[base], low))


def product_16(mats, base, value):
    return dot(mats[base], value) + dot(mats[base + 1], value)


def east_of(value):
    return pltpu.roll(value, LON - 1, 1)


def west_of(value):
    return pltpu.roll(value, 1, 1)


def kernel(
    lam_hbm, incr_hbm, winds_hbm, mixing_hbm, spread_hbm, vert_hbm, members_hbm, lam_out, incr_out,
    lam, incr, mixing, spread, vert, members,
    i6, l6, s6, w3, q_send, q_recv, lam_send, prop_send, arrived, fwd,
    mats, scaled, za, zb, ens,
    load_sem, tm_send, tm_recv, up_send, up_recv, dn_send, dn_recv, f_in, f_out, far_send,
):
    tm, lat = lax.axis_index("tm"), lax.axis_index("lat")
    place = lax.rem(lat, BAND)
    has_up, has_dn = lat < LAT - 1, lat > 0
    has_next, has_prev = tm < TM - 1, tm > 0
    cross_up = (place == BAND - 1) & has_up
    cross_dn = (place == 0) & has_dn

    is_even = lax.rem(tm, 2) == 0
    is_odd = jnp.logical_not(is_even)

    def at_place(kind, up):
        if up:
            return (place == PLACES[kind]) & (lat >= BAND)
        return (place == BAND - 1 - PLACES[kind]) & (lat < LAT - BAND)

    def of_tm(even):
        return is_even if even else is_odd

    def passes(kind, even, up):
        return at_place(kind, up) & of_tm(even)

    def straight(up):
        return is_even if up else is_odd

    def passes_dual(up):
        return at_place("seven", up) & straight(up) & has_next

    def sends_dual(up):
        return (cross_up if up else cross_dn) & jnp.logical_not(straight(up)) & has_prev

    loads = [
        pltpu.make_async_copy(src, dst, load_sem.at[at])
        for at, (src, dst) in enumerate(
            (
                (lam_hbm, lam),
                (spread_hbm, spread),
                (incr_hbm, incr),
                (winds_hbm, w3.at[1]),
                (members_hbm, members),
                (mixing_hbm, mixing),
                (vert_hbm, vert),
            )
        )
    ]
    for load in loads:
        load.start()

    barrier = pltpu.get_barrier_semaphore()
    greetings = [
        (has_next, {"tm": tm + 1}, has_prev),
        (has_prev, {"tm": tm - 1}, has_next),
        (has_up, {"lat": lat + 1}, has_dn),
        (has_dn, {"lat": lat - 1}, has_up),
        (passes_dual(True), {"tm": tm + 1, "lat": lat - PLACES["seven"] - 1}, sends_dual(True)),
        (passes_dual(False), {"tm": tm + 1, "lat": lat + PLACES["seven"] + 1}, sends_dual(False)),
    ]
    for kind, even in RELAYS:
        p = PLACES[kind]
        greetings += [
            (cross_up & of_tm(even), {"lat": lat - p}, passes(kind, even, False)),
            (cross_dn & of_tm(even), {"lat": lat + p}, passes(kind, even, True)),
            (passes(kind, even, True), {"lat": lat - p - 1}, cross_up & of_tm(even)),
            (passes(kind, even, False), {"lat": lat + p + 1}, cross_dn & of_tm(even)),
        ]
    targets = 0
    for cond, where, mirrored in greetings:
        targets = targets + jnp.where(mirrored, 1, 0)

        @pl.when(cond)
        def _():
            pl.semaphore_signal(barrier, inc=1, device_id=where, device_id_type=MESH)

    def ends(item, up):
        if item == WIN:
            return w3.at[1], w3.at[0 if up else 2]
        for first, buffer in ((INC, i6), (SCA, s6), (LNX, l6)):
            if first <= item < first + 2:
                row = item - first
                return buffer.at[2 + row], buffer.at[row if up else 4 + row]
        m = item - QEN
        return q_send.at[1 if up else 0, m], q_recv.at[0 if up else 1, m]

    def to_lat(item, up):
        src, dst = ends(item, up)
        send, recv = (up_send, up_recv) if up else (dn_send, dn_recv)
        where = {"lat": lat + 1 if up else lat - 1}
        return pltpu.make_async_remote_copy(
            src, dst, send.at[item], recv.at[item], device_id=where, device_id_type=MESH
        )

    def dual_across(row, up):
        where = {"tm": tm - 1, "lat": lat + BAND - 1 if up else lat - BAND + 1}
        return pltpu.make_async_remote_copy(
            lam_send.at[row], fwd.at[FAR + row], far_send.at[row], f_in.at[FAR + row],
            device_id=where, device_id_type=MESH,
        )

    def to_fwd(item, up, even):
        src, _ = ends(item, up)
        kind, at = route(item, even)
        send = up_send if up else dn_send
        p = PLACES[kind]
        where = {"lat": lat + p + 1 if up else lat - p - 1}
        return pltpu.make_async_remote_copy(
            src, fwd.at[at], send.at[item], f_in.at[at], device_id=where, device_id_type=MESH
        )

    def from_fwd(item, kind, at, up):
        _, dst = ends(item, up)
        recv = up_recv if up else dn_recv
        p = PLACES[kind]
        where = {"lat": lat - p if up else lat + p}
        return pltpu.make_async_remote_copy(
            fwd.at[at], dst, f_out.at[at], recv.at[item], device_id=where, device_id_type=MESH
        )

    def start_lat(items, cond=True, sides=(True, False)):
        for up, has, cross in ((True, has_up, cross_up), (False, has_dn, cross_dn)):
            if False in sides:

                @pl.when(has & jnp.logical_not(cross) & cond)
                def _():
                    for item in items:
                        to_lat(item, up).start()

            if True not in sides:
                continue
            for even in (True, False):

                @pl.when(cross & (is_even if even else is_odd) & cond)
                def _():
                    for item in items:
                        if route(item, even):
                            to_fwd(item, up, even).start()
                        elif item not in (LNX, LNX + 1) or even != up:
                            to_lat(item, up).start()

    def hand_over(item, kind, at, up):
        pltpu.make_async_remote_copy(
            fwd.at[at], fwd.at[at], f_out.at[at], f_in.at[at],
            device_id={"lat": lat - 1 if up else lat + 1}, device_id_type=MESH,
        ).wait_recv()
        from_fwd(item, kind, at, up).start()

    def pass_on(items, kinds=tuple(PLACES)):
        for kind, even in RELAYS:
            if kind not in kinds:
                continue
            now = [item for item in items if item in ROUTES[even][kind]]
            if not now:
                continue
            for up in (True, False):

                @pl.when(passes(kind, even, up))
                def _():
                    for item in now:
                        hand_over(item, kind, route(item, even)[1], up)

    def pass_duals():
        for up in (True, False):

            @pl.when(passes_dual(up))
            def _():
                for row in range(2):
                    hand_over(LNX + row, "seven", FAR + row, up)

    def await_lat(items, cond=True):
        for up, has in ((True, has_dn), (False, has_up)):

            @pl.when(has & cond)
            def _():
                for item in items:
                    to_lat(item, up).wait_recv()

    def dual_to_prev(row):
        return pltpu.make_async_remote_copy(
            lam_send.at[row], l6.at[2 + row], tm_send.at[row], tm_recv.at[row],
            device_id={"tm": tm - 1}, device_id_type=MESH,
        )

    def prop_to_next(row):
        return pltpu.make_async_remote_copy(
            prop_send.at[row], arrived.at[row], tm_send.at[2 + row], tm_recv.at[2 + row],
            device_id={"tm": tm + 1}, device_id_type=MESH,
        )

    for load in loads[:4]:
        load.wait()
    for row in range(2):
        for at, size in CHUNKS:
            rows = pl.ds(at, size)
            dual = lam[row, rows, :]
            product_now = spread[row, rows, :] * dual
            lam_send[row, rows, :] = dual.astype(BF16)
            i6[2 + row, rows, :] = incr[row, rows, :].astype(BF16)
            scaled[row, rows, :] = product_now
            s6[2 + row, rows, :] = product_now.astype(BF16)

    @pl.when(jnp.logical_not(has_dn))
    def _():
        w3[0] = jnp.zeros_like(w3[0])
        for buffer in (i6, l6, s6):
            for row in (0, 1):
                buffer[row] = jnp.zeros_like(buffer[row])
        for m in range(NENS):
            q_recv[0, m] = jnp.zeros_like(q_recv[0, m])

    @pl.when(jnp.logical_not(has_up))
    def _():
        w3[2] = jnp.zeros_like(w3[2])
        for buffer in (i6, l6, s6):
            for row in (4, 5):
                buffer[row] = jnp.zeros_like(buffer[row])
        for m in range(NENS):
            q_recv[1, m] = jnp.zeros_like(q_recv[1, m])

    @pl.when(jnp.logical_not(has_prev))
    def _():
        arrived[...] = jnp.zeros_like(arrived)

    pl.semaphore_wait(barrier, targets)

    @pl.when(has_prev)
    def _():
        dual_to_prev(0).start()
        dual_to_prev(1).start()

    start_lat([WIN, INC, INC + 1], has_next)
    start_lat([SCA, SCA + 1])
    for up in (True, False):

        @pl.when(sends_dual(up))
        def _():
            for row in range(2):
                dual_across(row, up).start()

    for load in loads[4:]:
        load.wait()
    for base, matrix in ((0, mixing[...]), (4, vert[...])):
        mats[base], mats[base + 1] = split(matrix)
        mats[base + 2], mats[base + 3] = split(matrix.T)

    for at, size in CHUNKS:
        rows = pl.ds(at, size)
        totals = [None, None]
        duals = [lam[row, rows, :] for row in range(2)]
        for m in range(NENS):
            perturb = [members[row, m, rows, :].astype(F32) for row in range(2)]
            weighted = [perturb[row] * duals[row] for row in range(2)]
            for row in range(2):
                q_send[row, m, rows, :] = weighted[row].astype(BF16)
                near = weighted[1 - row] + east_of(weighted[row]) + west_of(weighted[row])
                term = perturb[row] * (weighted[row] + 0.25 * near)
                totals[row] = term if m == 0 else totals[row] + term
        for row in range(2):
            ens[row, rows, :] = totals[row]

    edges = [QEN + m for m in range(NENS)]
    start_lat(edges, sides=(True,))
    start_lat(edges[:2], sides=(False,))
    def dual_row(row):
        @pl.when(has_next)
        def _():
            dual_to_prev(row).wait_recv()

        start_lat([LNX + row], has_next)

    pass_on([SCA, SCA + 1])
    pass_duals()
    dual_row(0)
    pass_on(edges, ("six",))
    dual_row(1)
    start_lat(edges[2:], sides=(False,))

    def weights(i):
        block, row = (i + 2) // 2, (i + 2) % 2
        north, south, east, west = (w3[block, p, row : row + 1, :] for p in range(4))
        return north, south, east, west, 1.0 - north - south - east - west

    low_edge = jnp.where(has_dn, 1.0, 0.0).astype(F32)
    high_edge = jnp.where(has_up, 1.0, 0.0).astype(F32)

    def inside(i, value):
        if i == -1:
            return value * low_edge
        if i == 2:
            return value * high_edge
        return value

    @pl.when(has_next)
    def _():
        await_lat([WIN, INC, INC + 1])

        def transport(of, i, rows):
            north, south, east, west, centre = weights(i)
            here = of(i, rows)
            total = centre * here + north * of(i + 1, rows) + south * of(i - 1, rows)
            return total + east * east_of(here) + west * west_of(here)

        def first(i, rows):
            if 0 <= i < 2:
                return incr[i, rows, :]
            return i6[i + 2, rows, :].astype(F32)

        for i in range(-1, 3):
            for at, size in CHUNKS:
                rows = pl.ds(at, size)
                za[i + 1, rows, :] = inside(i, transport(first, i, rows))
        for i in range(4):
            zb[i] = product(mats, 0, za[i])
        for i in range(2):
            for at, size in CHUNKS:
                rows = pl.ds(at, size)
                za[i, rows, :] = transport(lambda j, r: zb[j + 1, r, :], i, rows)
        for i in range(2):
            prop_send[i] = product(mats, 0, za[i]).astype(BF16)
            prop_to_next(i).start()

    pass_on(edges, ("seven", "one"))

    await_lat([SCA, SCA + 1])

    def smooth(of, i, rows):
        here = of(i, rows)
        return here + 0.25 * (of(i + 1, rows) + of(i - 1, rows) + east_of(here) + west_of(here))

    def field(i, rows):
        if 0 <= i < 2:
            return scaled[i, rows, :]
        return s6[i + 2, rows, :].astype(F32)

    for i in range(-1, 3):
        for at, size in CHUNKS:
            rows = pl.ds(at, size)
            za[i + 1, rows, :] = inside(i, smooth(field, i, rows))
    for i in range(2):
        for at, size in CHUNKS:
            rows = pl.ds(at, size)
            zb[i, rows, :] = smooth(lambda j, r: za[j + 1, r, :], i, rows)
    for i in range(2):
        za[i] = product(mats, 6, zb[i])
    for i in range(2):
        zb[i] = product(mats, 4, za[i])
    for i in range(2):
        for at, size in CHUNKS:
            rows = pl.ds(at, size)
            ens[i, rows, :] = (
                0.5 * (spread[i, rows, :] * zb[i, rows, :])
                + (0.5 / (NENS - 1)) * ens[i, rows, :]
                + incr[i, rows, :]
            )

    @pl.when(has_next)
    def _():
        await_lat([LNX, LNX + 1])

        def transport_back(of, i, rows):
            _, _, east, west, centre = weights(i)
            north, south = weights(i - 1)[0], weights(i + 1)[1]
            here = of(i, rows)
            total = centre * here + north * of(i - 1, rows) + south * of(i + 1, rows)
            return total + west_of(east * here) + east_of(west * here)

        for i in range(6):
            zb[i] = product_16(mats, 2, l6[i])
        for i in range(-1, 3):
            for at, size in CHUNKS:
                rows = pl.ds(at, size)
                za[i + 1, rows, :] = inside(
                    i, transport_back(lambda j, r: zb[j + 2, r, :], i, rows)
                )
        for i in range(4):
            zb[i] = product(mats, 2, za[i])
        for i in range(2):
            for at, size in CHUNKS:
                rows = pl.ds(at, size)
                back = transport_back(lambda j, r: zb[j + 1, r, :], i, rows)
                incr_out[i, rows, :] = lam[i, rows, :] - back

    @pl.when(jnp.logical_not(has_next))
    def _():
        incr_out[...] = lam[...]

    await_lat(edges)

    @pl.when(has_prev)
    def _():
        prop_from = [
            pltpu.make_async_remote_copy(
                prop_send.at[row], arrived.at[row], tm_send.at[2 + row], tm_recv.at[2 + row],
                device_id={"tm": tm - 1}, device_id_type=MESH,
            )
            for row in range(2)
        ]
        for copy in prop_from:
            copy.wait_recv()

    for i in range(2):
        for at, size in CHUNKS:
            rows = pl.ds(at, size)
            near = None
            for m in range(NENS):
                term = members[i, m, rows, :].astype(F32) * q_recv[i, m, rows, :].astype(F32)
                near = term if m == 0 else near + term
            lam_out[i, rows, :] = (
                ens[i, rows, :]
                + (0.5 * 0.25 / (NENS - 1)) * near
                - arrived[i, rows, :].astype(F32)
            )

    @pl.when(has_prev)
    def _():
        dual_to_prev(0).wait_send()
        dual_to_prev(1).wait_send()

    @pl.when(has_next)
    def _():
        prop_to_next(0).wait_send()
        prop_to_next(1).wait_send()

    for up, has, cross in ((True, has_up, cross_up), (False, has_dn, cross_dn)):

        @pl.when(has)
        def _():
            for item in [SCA, SCA + 1, *edges]:
                to_lat(item, up).wait_send()

        @pl.when(has & has_next)
        def _():
            for item in [WIN, INC, INC + 1]:
                to_lat(item, up).wait_send()

        @pl.when(has & has_next & (jnp.logical_not(cross) | jnp.logical_not(straight(up))))
        def _():
            for item in [LNX, LNX + 1]:
                to_lat(item, up).wait_send()

        @pl.when(sends_dual(up))
        def _():
            for row in range(2):
                dual_across(row, up).wait_send()

        for kind, even in RELAYS:

            @pl.when(passes(kind, even, up))
            def _():
                for at, item in enumerate(ROUTES[even][kind]):
                    from_fwd(item, kind, at, up).wait_send()

        @pl.when(passes_dual(up))
        def _():
            for row in range(2):
                from_fwd(LNX + row, "seven", FAR + row, up).wait_send()


def per_device(lam, incr, winds, mixing, spread, vert_corr, members):
    row = (COMP, LON)
    vmem = pl.BlockSpec(memory_space=pltpu.VMEM)
    state = jax.ShapeDtypeStruct((2, *row), F32)
    dma = pltpu.SemaphoreType.DMA
    scratch = [
        pltpu.VMEM((2, *row), F32),
        pltpu.VMEM((2, *row), F32),
        pltpu.VMEM((COMP, COMP), F32),
        pltpu.VMEM((2, *row), F32),
        pltpu.VMEM((COMP, COMP), F32),
        pltpu.VMEM((2, NENS, *row), BF16),
        pltpu.VMEM((6, *row), BF16),
        pltpu.VMEM((6, *row), BF16),
        pltpu.VMEM((6, *row), BF16),
        pltpu.VMEM((3, 4, 2, LON), F32),
        pltpu.VMEM((2, NENS, *row), BF16),
        pltpu.VMEM((2, NENS, *row), BF16),
        pltpu.VMEM((2, *row), BF16),
        pltpu.VMEM((2, *row), BF16),
        pltpu.VMEM((2, *row), BF16),
        pltpu.VMEM((SLOTS, *row), BF16),
        pltpu.VMEM((8, COMP, COMP), BF16),
        pltpu.VMEM((2, *row), F32),
        pltpu.VMEM((4, *row), F32),
        pltpu.VMEM((6, *row), F32),
        pltpu.VMEM((2, *row), F32),
        dma((7,)),
        dma((4,)),
        dma((4,)),
        dma((ITEMS,)),
        dma((ITEMS,)),
        dma((ITEMS,)),
        dma((ITEMS,)),
        dma((SLOTS,)),
        dma((SLOTS,)),
        dma((2,)),
    ]
    lam_result, incr_result = pl.pallas_call(
        kernel,
        out_shape=(state, state),
        in_specs=[pl.BlockSpec(memory_space=pltpu.HBM)] * 7,
        out_specs=(vmem, vmem),
        scratch_shapes=scratch,
        compiler_params=pltpu.CompilerParams(
            collective_id=0, has_side_effects=True, vmem_limit_bytes=48 * 2**20
        ),
    )(
        *(
            pltpu.with_memory_space_constraint(array, pltpu.HBM)
            for array in (lam[0], incr[0], winds[0], mixing[0], spread[0], vert_corr, members[0])
        )
    )
    return lam_result[None], incr_result[None]


def solution(mesh):
    in_specs = (
        P("tm", "lat", None, None),
        P("tm", "lat", None, None),
        P("tm", None, "lat", None),
        P("tm", None, None),
        P("tm", "lat", None, None),
        P(),
        P("tm", "lat", None, None, None),
    )
    out_specs = (P("tm", "lat", None, None), P("tm", "lat", None, None))
    return jax.shard_map(
        per_device, mesh=mesh, in_specs=in_specs, out_specs=out_specs, check_vma=False
    )
```

```python
import jax
import jax.numpy as jnp
from jax import lax
from jax.experimental import pallas as pl
from jax.experimental.pallas import tpu as pltpu
from jax.sharding import PartitionSpec as P

MESH = pl.DeviceIdType.MESH
F32, BF16 = jnp.float32, jnp.bfloat16
COMP, LON, NENS = 216, 256, 4
TM, LAT, BAND = 8, 64, 16
CHUNKS = [(at, min(32, COMP - at)) for at in range(0, COMP, 32)]

WIN, INC, SCA, LNX, QEN = 0, 1, 3, 5, 7
ITEMS = 11
PLACES = {"seven": 14, "six": 12, "one": 2}
ROUTES = {
    True: {"seven": (SCA, SCA + 1, QEN), "six": (QEN + 2, QEN + 3)},
    False: {"seven": (QEN, QEN + 1), "one": (SCA, SCA + 1, QEN + 2, QEN + 3)},
}
RELAYS = [(kind, even) for even, kinds in ROUTES.items() for kind in kinds]
FAR = 4
SLOTS = FAR + 2


def route(item, even):
    for kind, items in ROUTES[even].items():
        if item in items:
            return kind, items.index(item)
    return None


def split(value):
    high = value.astype(BF16)
    return high, (value - high.astype(F32)).astype(BF16)


def dot(a, b):
    return jnp.dot(a, b, preferred_element_type=F32)


def product(mats, base, value):
    high, low = split(value)
    return dot(mats[base], high) + (dot(mats[base + 1], high) + dot(mats[base], low))


def product_16(mats, base, value):
    return dot(mats[base], value) + dot(mats[base + 1], value)


def east_of(value):
    return pltpu.roll(value, LON - 1, 1)


def west_of(value):
    return pltpu.roll(value, 1, 1)


def kernel(
    lam_hbm, incr_hbm, winds_hbm, mixing_hbm, spread_hbm, vert_hbm, members_hbm, lam_out, incr_out,
    lam, incr, mixing, spread, vert, members,
    i6, l6, s6, w3, q_send, q_recv, lam_send, prop_send, arrived, fwd,
    mats, scaled, ya, za, zb, ens,
    load_sem, tm_send, tm_recv, up_send, up_recv, dn_send, dn_recv, f_in, f_out, far_send,
):
    tm, lat = lax.axis_index("tm"), lax.axis_index("lat")
    place = lax.rem(lat, BAND)
    has_up, has_dn = lat < LAT - 1, lat > 0
    has_next, has_prev = tm < TM - 1, tm > 0
    cross_up = (place == BAND - 1) & has_up
    cross_dn = (place == 0) & has_dn

    is_even = lax.rem(tm, 2) == 0
    is_odd = jnp.logical_not(is_even)

    def at_place(kind, up):
        if up:
            return (place == PLACES[kind]) & (lat >= BAND)
        return (place == BAND - 1 - PLACES[kind]) & (lat < LAT - BAND)

    def of_tm(even):
        return is_even if even else is_odd

    def passes(kind, even, up):
        return at_place(kind, up) & of_tm(even)

    def straight(up):
        return is_even if up else is_odd

    def passes_dual(up):
        return at_place("seven", up) & straight(up) & has_next

    first_duals = (cross_up & is_odd) | (cross_dn & is_even)

    def sends_dual(up):
        return (cross_up if up else cross_dn) & jnp.logical_not(straight(up)) & has_prev

    barrier = pltpu.get_barrier_semaphore()
    greetings = [
        (has_next, {"tm": tm + 1}, has_prev),
        (has_prev, {"tm": tm - 1}, has_next),
        (has_up, {"lat": lat + 1}, has_dn),
        (has_dn, {"lat": lat - 1}, has_up),
        (passes_dual(True), {"tm": tm + 1, "lat": lat - PLACES["seven"] - 1}, sends_dual(True)),
        (passes_dual(False), {"tm": tm + 1, "lat": lat + PLACES["seven"] + 1}, sends_dual(False)),
    ]
    for kind, even in RELAYS:
        p = PLACES[kind]
        greetings += [
            (cross_up & of_tm(even), {"lat": lat - p}, passes(kind, even, False)),
            (cross_dn & of_tm(even), {"lat": lat + p}, passes(kind, even, True)),
            (passes(kind, even, True), {"lat": lat - p - 1}, cross_up & of_tm(even)),
            (passes(kind, even, False), {"lat": lat + p + 1}, cross_dn & of_tm(even)),
        ]
    targets = 0
    for cond, where, mirrored in greetings:
        targets = targets + jnp.where(mirrored, 1, 0)

        @pl.when(cond)
        def _():
            pl.semaphore_signal(barrier, inc=1, device_id=where, device_id_type=MESH)

    loads = [
        pltpu.make_async_copy(src, dst, load_sem.at[at])
        for at, (src, dst) in enumerate(
            (
                (lam_hbm, lam),
                (spread_hbm, spread),
                (incr_hbm, incr),
                (winds_hbm, w3.at[1]),
                (members_hbm, members),
                (mixing_hbm, mixing),
                (vert_hbm, vert),
            )
        )
    ]
    for load in loads:
        load.start()

    def ends(item, up):
        if item == WIN:
            return w3.at[1], w3.at[0 if up else 2]
        for first, buffer in ((INC, i6), (SCA, s6), (LNX, l6)):
            if first <= item < first + 2:
                row = item - first
                return buffer.at[2 + row], buffer.at[row if up else 4 + row]
        m = item - QEN
        return q_send.at[1 if up else 0, m], q_recv.at[0 if up else 1, m]

    def to_lat(item, up):
        src, dst = ends(item, up)
        send, recv = (up_send, up_recv) if up else (dn_send, dn_recv)
        where = {"lat": lat + 1 if up else lat - 1}
        return pltpu.make_async_remote_copy(
            src, dst, send.at[item], recv.at[item], device_id=where, device_id_type=MESH
        )

    def dual_across(row, up):
        where = {"tm": tm - 1, "lat": lat + BAND - 1 if up else lat - BAND + 1}
        return pltpu.make_async_remote_copy(
            lam_send.at[row], fwd.at[FAR + row], far_send.at[row], f_in.at[FAR + row],
            device_id=where, device_id_type=MESH,
        )

    def to_fwd(item, up, even):
        src, _ = ends(item, up)
        kind, at = route(item, even)
        send = up_send if up else dn_send
        p = PLACES[kind]
        where = {"lat": lat + p + 1 if up else lat - p - 1}
        return pltpu.make_async_remote_copy(
            src, fwd.at[at], send.at[item], f_in.at[at], device_id=where, device_id_type=MESH
        )

    def from_fwd(item, kind, at, up):
        _, dst = ends(item, up)
        recv = up_recv if up else dn_recv
        p = PLACES[kind]
        where = {"lat": lat - p if up else lat + p}
        return pltpu.make_async_remote_copy(
            fwd.at[at], dst, f_out.at[at], recv.at[item], device_id=where, device_id_type=MESH
        )

    def start_lat(items, cond=True, sides=(True, False)):
        for up, has, cross in ((True, has_up, cross_up), (False, has_dn, cross_dn)):
            if False in sides:

                @pl.when(has & jnp.logical_not(cross) & cond)
                def _():
                    for item in items:
                        to_lat(item, up).start()

            if True not in sides:
                continue
            for even in (True, False):

                @pl.when(cross & (is_even if even else is_odd) & cond)
                def _():
                    for item in items:
                        if route(item, even):
                            to_fwd(item, up, even).start()
                        elif item not in (LNX, LNX + 1) or even != up:
                            to_lat(item, up).start()

    def hand_over(item, kind, at, up):
        pltpu.make_async_remote_copy(
            fwd.at[at], fwd.at[at], f_out.at[at], f_in.at[at],
            device_id={"lat": lat - 1 if up else lat + 1}, device_id_type=MESH,
        ).wait_recv()
        from_fwd(item, kind, at, up).start()

    def pass_on(items, kinds=tuple(PLACES)):
        for kind, even in RELAYS:
            if kind not in kinds:
                continue
            now = [item for item in items if item in ROUTES[even][kind]]
            if not now:
                continue
            for up in (True, False):

                @pl.when(passes(kind, even, up))
                def _():
                    for item in now:
                        hand_over(item, kind, route(item, even)[1], up)

    def pass_duals():
        for up in (True, False):

            @pl.when(passes_dual(up))
            def _():
                for row in range(2):
                    hand_over(LNX + row, "seven", FAR + row, up)

    def await_lat(items, cond=True):
        for up, has in ((True, has_dn), (False, has_up)):

            @pl.when(has & cond)
            def _():
                for item in items:
                    to_lat(item, up).wait_recv()

    def dual_to_prev(row):
        return pltpu.make_async_remote_copy(
            lam_send.at[row], l6.at[2 + row], tm_send.at[row], tm_recv.at[row],
            device_id={"tm": tm - 1}, device_id_type=MESH,
        )

    def prop_to_next(row):
        return pltpu.make_async_remote_copy(
            prop_send.at[row], arrived.at[row], tm_send.at[2 + row], tm_recv.at[2 + row],
            device_id={"tm": tm + 1}, device_id_type=MESH,
        )

    for load in loads[:4]:
        load.wait()
    for row in range(2):
        for at, size in CHUNKS:
            rows = pl.ds(at, size)
            dual = lam[row, rows, :]
            product_now = spread[row, rows, :] * dual
            lam_send[row, rows, :] = dual.astype(BF16)
            i6[2 + row, rows, :] = incr[row, rows, :].astype(BF16)
            scaled[row, rows, :] = product_now
            s6[2 + row, rows, :] = product_now.astype(BF16)

    @pl.when(jnp.logical_not(has_dn))
    def _():
        w3[0] = jnp.zeros_like(w3[0])
        for buffer in (i6, l6, s6):
            for row in (0, 1):
                buffer[row] = jnp.zeros_like(buffer[row])
        for m in range(NENS):
            q_recv[0, m] = jnp.zeros_like(q_recv[0, m])

    @pl.when(jnp.logical_not(has_up))
    def _():
        w3[2] = jnp.zeros_like(w3[2])
        for buffer in (i6, l6, s6):
            for row in (4, 5):
                buffer[row] = jnp.zeros_like(buffer[row])
        for m in range(NENS):
            q_recv[1, m] = jnp.zeros_like(q_recv[1, m])

    @pl.when(jnp.logical_not(has_prev))
    def _():
        arrived[...] = jnp.zeros_like(arrived)

    pl.semaphore_wait(barrier, targets)

    @pl.when(has_prev)
    def _():
        dual_to_prev(0).start()
        dual_to_prev(1).start()

    start_lat([WIN, INC, INC + 1], has_next)
    start_lat([SCA, SCA + 1])
    for up in (True, False):

        @pl.when(sends_dual(up))
        def _():
            for row in range(2):
                dual_across(row, up).start()

    for load in loads[4:]:
        load.wait()
    mats[0], mats[1] = split(mixing[...])
    mats[2], mats[3] = split(mixing[...].T)
    high, low = split(vert[...])
    high_t, low_t = split(vert[...].T)
    mats[4], mats[5] = split(dot(high, high_t) + (dot(high, low_t) + dot(low, high_t)))

    for at, size in CHUNKS:
        rows = pl.ds(at, size)
        totals = [None, None]
        duals = [lam[row, rows, :] for row in range(2)]
        for m in range(NENS):
            perturb = [members[row, m, rows, :].astype(F32) for row in range(2)]
            weighted = [perturb[row] * duals[row] for row in range(2)]
            for row in range(2):
                q_send[row, m, rows, :] = weighted[row].astype(BF16)
                near = weighted[1 - row] + east_of(weighted[row]) + west_of(weighted[row])
                term = perturb[row] * (weighted[row] + 0.25 * near)
                totals[row] = term if m == 0 else totals[row] + term
        for row in range(2):
            ens[row, rows, :] = (0.5 / (NENS - 1)) * totals[row] + incr[row, rows, :]

    edges = [QEN + m for m in range(NENS)]
    start_lat(edges, sides=(True,))
    start_lat(edges[:2], sides=(False,))
    def dual_row(row, cond=True):
        @pl.when(has_next & cond)
        def _():
            dual_to_prev(row).wait_recv()

        start_lat([LNX + row], has_next & cond)

    pass_on([SCA, SCA + 1], ("seven",))
    pass_duals()
    for row in range(2):
        dual_row(row, first_duals)

    def weights(i):
        block, row = (i + 2) // 2, (i + 2) % 2
        north, south, east, west = (w3[block, p, row : row + 1, :] for p in range(4))
        return north, south, east, west, 1.0 - north - south - east - west

    low_edge = jnp.where(has_dn, 1.0, 0.0).astype(F32)
    high_edge = jnp.where(has_up, 1.0, 0.0).astype(F32)

    def inside(i, value):
        if i == -1:
            return value * low_edge
        if i == 2:
            return value * high_edge
        return value

    @pl.when(has_next)
    def _():
        await_lat([WIN, INC, INC + 1])

        def transport(of, i, rows):
            north, south, east, west, centre = weights(i)
            here = of(i, rows)
            total = centre * here + north * of(i + 1, rows) + south * of(i - 1, rows)
            return total + east * east_of(here) + west * west_of(here)

        def first(i, rows):
            if 0 <= i < 2:
                return incr[i, rows, :]
            return i6[i + 2, rows, :].astype(F32)

        for i in range(-1, 3):
            for at, size in CHUNKS:
                rows = pl.ds(at, size)
                za[i + 1, rows, :] = inside(i, transport(first, i, rows))
        for i in range(4):
            zb[i] = product(mats, 0, za[i])
        for i in range(2):
            for at, size in CHUNKS:
                rows = pl.ds(at, size)
                za[i, rows, :] = transport(lambda j, r: zb[j + 1, r, :], i, rows)
        for i in range(2):
            prop_send[i] = product(mats, 0, za[i]).astype(BF16)
            prop_to_next(i).start()

    dual_row(0, jnp.logical_not(first_duals))
    pass_on(edges, ("six",))
    dual_row(1, jnp.logical_not(first_duals))
    start_lat(edges[2:], sides=(False,))
    pass_on([SCA, SCA + 1], ("one",))
    pass_on(edges, ("seven", "one"))

    early_edges = cross_up & is_even

    def add_edges(cond):
        await_lat(edges, cond)

        @pl.when(cond)
        def _():
            for i in range(2):
                for at, size in CHUNKS:
                    rows = pl.ds(at, size)
                    near = None
                    for m in range(NENS):
                        term = members[i, m, rows, :].astype(F32) * q_recv[i, m, rows, :].astype(F32)
                        near = term if m == 0 else near + term
                    ens[i, rows, :] += (0.5 * 0.25 / (NENS - 1)) * near

    @pl.when(has_next)
    def _():
        for i in (2, 3):
            ya[i] = product_16(mats, 2, l6[i])

    add_edges(early_edges)

    await_lat([SCA, SCA + 1])

    def smooth(of, i, rows):
        here = of(i, rows)
        return here + 0.25 * (of(i + 1, rows) + of(i - 1, rows) + east_of(here) + west_of(here))

    def field(i, rows):
        if 0 <= i < 2:
            return scaled[i, rows, :]
        return s6[i + 2, rows, :].astype(F32)

    for i in range(-1, 3):
        for at, size in CHUNKS:
            rows = pl.ds(at, size)
            za[i + 1, rows, :] = inside(i, smooth(field, i, rows))
    for i in range(2):
        for at, size in CHUNKS:
            rows = pl.ds(at, size)
            zb[i, rows, :] = smooth(lambda j, r: za[j + 1, r, :], i, rows)
    for i in range(2):
        za[i] = product(mats, 4, zb[i])
        for at, size in CHUNKS:
            rows = pl.ds(at, size)
            ens[i, rows, :] += 0.5 * (spread[i, rows, :] * za[i, rows, :])

    @pl.when(has_next)
    def _():
        await_lat([LNX, LNX + 1])

        def transport_back(of, i, rows):
            _, _, east, west, centre = weights(i)
            north, south = weights(i - 1)[0], weights(i + 1)[1]
            here = of(i, rows)
            total = centre * here + north * of(i - 1, rows) + south * of(i + 1, rows)
            return total + west_of(east * here) + east_of(west * here)

        for i in (0, 1, 4, 5):
            ya[i] = product_16(mats, 2, l6[i])
        for i in range(-1, 3):
            for at, size in CHUNKS:
                rows = pl.ds(at, size)
                za[i + 1, rows, :] = inside(
                    i, transport_back(lambda j, r: ya[j + 2, r, :], i, rows)
                )
        for i in range(4):
            zb[i] = product(mats, 2, za[i])
        for i in range(2):
            for at, size in CHUNKS:
                rows = pl.ds(at, size)
                back = transport_back(lambda j, r: zb[j + 1, r, :], i, rows)
                incr_out[i, rows, :] = lam[i, rows, :] - back

    @pl.when(jnp.logical_not(has_next))
    def _():
        incr_out[...] = lam[...]

    add_edges(jnp.logical_not(early_edges))

    @pl.when(has_prev)
    def _():
        prop_from = [
            pltpu.make_async_remote_copy(
                prop_send.at[row], arrived.at[row], tm_send.at[2 + row], tm_recv.at[2 + row],
                device_id={"tm": tm - 1}, device_id_type=MESH,
            )
            for row in range(2)
        ]
        for copy in prop_from:
            copy.wait_recv()

    for i in range(2):
        for at, size in CHUNKS:
            rows = pl.ds(at, size)
            lam_out[i, rows, :] = ens[i, rows, :] - arrived[i, rows, :].astype(F32)

    @pl.when(has_prev)
    def _():
        dual_to_prev(0).wait_send()
        dual_to_prev(1).wait_send()

    @pl.when(has_next)
    def _():
        prop_to_next(0).wait_send()
        prop_to_next(1).wait_send()

    for up, has, cross in ((True, has_up, cross_up), (False, has_dn, cross_dn)):

        @pl.when(has)
        def _():
            for item in [SCA, SCA + 1, *edges]:
                to_lat(item, up).wait_send()

        @pl.when(has & has_next)
        def _():
            for item in [WIN, INC, INC + 1]:
                to_lat(item, up).wait_send()

        @pl.when(has & has_next & (jnp.logical_not(cross) | jnp.logical_not(straight(up))))
        def _():
            for item in [LNX, LNX + 1]:
                to_lat(item, up).wait_send()

        @pl.when(sends_dual(up))
        def _():
            for row in range(2):
                dual_across(row, up).wait_send()

        for kind, even in RELAYS:

            @pl.when(passes(kind, even, up))
            def _():
                for at, item in enumerate(ROUTES[even][kind]):
                    from_fwd(item, kind, at, up).wait_send()

        @pl.when(passes_dual(up))
        def _():
            for row in range(2):
                from_fwd(LNX + row, "seven", FAR + row, up).wait_send()


def per_device(lam, incr, winds, mixing, spread, vert_corr, members):
    row = (COMP, LON)
    vmem = pl.BlockSpec(memory_space=pltpu.VMEM)
    state = jax.ShapeDtypeStruct((2, *row), F32)
    dma = pltpu.SemaphoreType.DMA
    scratch = [
        pltpu.VMEM((2, *row), F32),
        pltpu.VMEM((2, *row), F32),
        pltpu.VMEM((COMP, COMP), F32),
        pltpu.VMEM((2, *row), F32),
        pltpu.VMEM((COMP, COMP), F32),
        pltpu.VMEM((2, NENS, *row), BF16),
        pltpu.VMEM((6, *row), BF16),
        pltpu.VMEM((6, *row), BF16),
        pltpu.VMEM((6, *row), BF16),
        pltpu.VMEM((3, 4, 2, LON), F32),
        pltpu.VMEM((2, NENS, *row), BF16),
        pltpu.VMEM((2, NENS, *row), BF16),
        pltpu.VMEM((2, *row), BF16),
        pltpu.VMEM((2, *row), BF16),
        pltpu.VMEM((2, *row), BF16),
        pltpu.VMEM((SLOTS, *row), BF16),
        pltpu.VMEM((6, COMP, COMP), BF16),
        pltpu.VMEM((2, *row), F32),
        pltpu.VMEM((6, *row), F32),
        pltpu.VMEM((4, *row), F32),
        pltpu.VMEM((4, *row), F32),
        pltpu.VMEM((2, *row), F32),
        dma((7,)),
        dma((4,)),
        dma((4,)),
        dma((ITEMS,)),
        dma((ITEMS,)),
        dma((ITEMS,)),
        dma((ITEMS,)),
        dma((SLOTS,)),
        dma((SLOTS,)),
        dma((2,)),
    ]
    lam_result, incr_result = pl.pallas_call(
        kernel,
        out_shape=(state, state),
        in_specs=[pl.BlockSpec(memory_space=pltpu.HBM)] * 7,
        out_specs=(vmem, vmem),
        scratch_shapes=scratch,
        compiler_params=pltpu.CompilerParams(
            collective_id=0, has_side_effects=True, vmem_limit_bytes=48 * 2**20
        ),
    )(
        *(
            pltpu.with_memory_space_constraint(array, pltpu.HBM)
            for array in (lam[0], incr[0], winds[0], mixing[0], spread[0], vert_corr, members[0])
        )
    )
    return lam_result[None], incr_result[None]


def solution(mesh):
    in_specs = (
        P("tm", "lat", None, None),
        P("tm", "lat", None, None),
        P("tm", None, "lat", None),
        P("tm", None, None),
        P("tm", "lat", None, None),
        P(),
        P("tm", "lat", None, None, None),
    )
    out_specs = (P("tm", "lat", None, None), P("tm", "lat", None, None))
    return jax.shard_map(
        per_device, mesh=mesh, in_specs=in_specs, out_specs=out_specs, check_vma=False
    )
```

```python
import jax
import jax.numpy as jnp
from jax import lax
from jax.experimental import pallas as pl
from jax.experimental.pallas import tpu as pltpu
from jax.sharding import PartitionSpec as P

MESH = pl.DeviceIdType.MESH
F32, BF16 = jnp.float32, jnp.bfloat16
COMP, LON, NENS = 216, 256, 4
HALF = LON // 2
TM, LAT, BAND = 8, 64, 16
CHUNKS = [(at, min(32, COMP - at)) for at in range(0, COMP, 32)]

WIN, INC, SCA, LNX, MEM, DUAL, BACK = 0, 1, 3, 5, 7, 9, 10
ITEMS = 11
PLACES = {"seven": 14, "six": 12, "one": 2}
ROUTES = {
    True: {"seven": (SCA, SCA + 1, MEM), "six": (MEM + 1, DUAL)},
    False: {"seven": (MEM,), "one": (SCA, SCA + 1, MEM + 1, DUAL)},
}
RELAYS = [(kind, even) for even, kinds in ROUTES.items() for kind in kinds]
FAR = 4
SLOTS = FAR + 2


def route(item, even):
    for kind, items in ROUTES[even].items():
        if item in items:
            return kind, items.index(item)
    return None


def split(value):
    high = value.astype(BF16)
    return high, (value - high.astype(F32)).astype(BF16)


def dot(a, b):
    return jnp.dot(a, b, preferred_element_type=F32)


def product(mats, base, value):
    high, low = split(value)
    return dot(mats[base], high) + (dot(mats[base + 1], high) + dot(mats[base], low))


def product_16(mats, base, value):
    return dot(mats[base], value) + dot(mats[base + 1], value)


def east_of(value):
    return pltpu.roll(value, LON - 1, 1)


def west_of(value):
    return pltpu.roll(value, 1, 1)


def kernel(
    lam_hbm, incr_hbm, winds_hbm, mixing_hbm, spread_hbm, vert_hbm, members_hbm, lam_out, incr_out,
    lam, incr, mixing, spread, vert, members,
    i6, l6, s6, w3, p_recv, d_recv, b_send, b_recv, lam_send, prop_send, arrived, fwd, fwd_p, fwd_d,
    mats, scaled, ya, za, zb, ens,
    load_sem, tm_send, tm_recv, up_send, up_recv, dn_send, dn_recv, f_in, f_out, far_send,
):
    tm, lat = lax.axis_index("tm"), lax.axis_index("lat")
    place = lax.rem(lat, BAND)
    has_up, has_dn = lat < LAT - 1, lat > 0
    has_next, has_prev = tm < TM - 1, tm > 0
    cross_up = (place == BAND - 1) & has_up
    cross_dn = (place == 0) & has_dn

    is_even = lax.rem(tm, 2) == 0
    is_odd = jnp.logical_not(is_even)

    def at_place(kind, up):
        if up:
            return (place == PLACES[kind]) & (lat >= BAND)
        return (place == BAND - 1 - PLACES[kind]) & (lat < LAT - BAND)

    def of_tm(even):
        return is_even if even else is_odd

    def passes(kind, even, up):
        return at_place(kind, up) & of_tm(even)

    def straight(up):
        return is_even if up else is_odd

    def passes_dual(up):
        return at_place("seven", up) & straight(up) & has_next

    first_duals = (cross_up & is_odd) | (cross_dn & is_even)

    def sends_dual(up):
        return (cross_up if up else cross_dn) & jnp.logical_not(straight(up)) & has_prev

    barrier = pltpu.get_barrier_semaphore()
    greetings = [
        (has_next, {"tm": tm + 1}, has_prev),
        (has_prev, {"tm": tm - 1}, has_next),
        (has_up, {"lat": lat + 1}, has_dn),
        (has_dn, {"lat": lat - 1}, has_up),
        (passes_dual(True), {"tm": tm + 1, "lat": lat - PLACES["seven"] - 1}, sends_dual(True)),
        (passes_dual(False), {"tm": tm + 1, "lat": lat + PLACES["seven"] + 1}, sends_dual(False)),
    ]
    for kind, even in RELAYS:
        p = PLACES[kind]
        greetings += [
            (cross_up & of_tm(even), {"lat": lat - p}, passes(kind, even, False)),
            (cross_dn & of_tm(even), {"lat": lat + p}, passes(kind, even, True)),
            (passes(kind, even, True), {"lat": lat - p - 1}, cross_up & of_tm(even)),
            (passes(kind, even, False), {"lat": lat + p + 1}, cross_dn & of_tm(even)),
        ]
    targets = 0
    for cond, where, mirrored in greetings:
        targets = targets + jnp.where(mirrored, 1, 0)

        @pl.when(cond)
        def _():
            pl.semaphore_signal(barrier, inc=1, device_id=where, device_id_type=MESH)

    loads = [
        pltpu.make_async_copy(src, dst, load_sem.at[at])
        for at, (src, dst) in enumerate(
            (
                (lam_hbm, lam),
                (spread_hbm, spread),
                (incr_hbm, incr),
                (winds_hbm, w3.at[1]),
                (members_hbm, members),
                (mixing_hbm, mixing),
                (vert_hbm, vert),
            )
        )
    ]
    for load in loads:
        load.start()

    def ends(item, up):
        if item == WIN:
            return w3.at[1], w3.at[0 if up else 2]
        for first, buffer in ((INC, i6), (SCA, s6), (LNX, l6)):
            if first <= item < first + 2:
                row = item - first
                return buffer.at[2 + row], buffer.at[row if up else 4 + row]
        row, side, half = (1, 0, pl.ds(0, HALF)) if up else (0, 1, pl.ds(HALF, HALF))
        if item == DUAL:
            return lam_send.at[row, :, half], d_recv.at[side]
        if item == BACK:
            return b_send.at[row], b_recv.at[side]
        pair = pl.ds(2 * (item - MEM), 2)
        return members.at[row, pair, :, half], p_recv.at[side, pair]

    def slot(item, at):
        if item in (MEM, MEM + 1):
            return fwd_p.at[item - MEM]
        return fwd_d if item == DUAL else fwd.at[at]

    def to_lat(item, up):
        src, dst = ends(item, up)
        send, recv = (up_send, up_recv) if up else (dn_send, dn_recv)
        where = {"lat": lat + 1 if up else lat - 1}
        return pltpu.make_async_remote_copy(
            src, dst, send.at[item], recv.at[item], device_id=where, device_id_type=MESH
        )

    def dual_across(row, up):
        where = {"tm": tm - 1, "lat": lat + BAND - 1 if up else lat - BAND + 1}
        return pltpu.make_async_remote_copy(
            lam_send.at[row], fwd.at[FAR + row], far_send.at[row], f_in.at[FAR + row],
            device_id=where, device_id_type=MESH,
        )

    def to_fwd(item, up, even):
        src, _ = ends(item, up)
        kind, at = route(item, even)
        send = up_send if up else dn_send
        p = PLACES[kind]
        where = {"lat": lat + p + 1 if up else lat - p - 1}
        return pltpu.make_async_remote_copy(
            src, slot(item, at), send.at[item], f_in.at[at], device_id=where, device_id_type=MESH
        )

    def from_fwd(item, kind, at, up):
        _, dst = ends(item, up)
        recv = up_recv if up else dn_recv
        p = PLACES[kind]
        where = {"lat": lat - p if up else lat + p}
        return pltpu.make_async_remote_copy(
            slot(item, at), dst, f_out.at[at], recv.at[item], device_id=where, device_id_type=MESH
        )

    def start_lat(items, cond=True, sides=(True, False)):
        for up, has, cross in ((True, has_up, cross_up), (False, has_dn, cross_dn)):
            if False in sides:

                @pl.when(has & jnp.logical_not(cross) & cond)
                def _():
                    for item in items:
                        to_lat(item, up).start()

            if True not in sides:
                continue
            for even in (True, False):

                @pl.when(cross & (is_even if even else is_odd) & cond)
                def _():
                    for item in items:
                        if route(item, even):
                            to_fwd(item, up, even).start()
                        elif item not in (LNX, LNX + 1) or even != up:
                            to_lat(item, up).start()

    def hand_over(item, kind, at, up):
        pltpu.make_async_remote_copy(
            slot(item, at), slot(item, at), f_out.at[at], f_in.at[at],
            device_id={"lat": lat - 1 if up else lat + 1}, device_id_type=MESH,
        ).wait_recv()
        from_fwd(item, kind, at, up).start()

    def pass_on(items, kinds, parities=(True, False)):
        for kind, even in RELAYS:
            if kind not in kinds or even not in parities:
                continue
            now = [item for item in items if item in ROUTES[even][kind]]
            if not now:
                continue
            for up in (True, False):

                @pl.when(passes(kind, even, up))
                def _():
                    for item in now:
                        hand_over(item, kind, route(item, even)[1], up)

    def pass_duals():
        for up in (True, False):

            @pl.when(passes_dual(up))
            def _():
                for row in range(2):
                    hand_over(LNX + row, "seven", FAR + row, up)

    def await_lat(items, cond=True):
        for up, has in ((True, has_dn), (False, has_up)):

            @pl.when(has & cond)
            def _():
                for item in items:
                    to_lat(item, up).wait_recv()

    def dual_to_prev(row):
        return pltpu.make_async_remote_copy(
            lam_send.at[row], l6.at[2 + row], tm_send.at[row], tm_recv.at[row],
            device_id={"tm": tm - 1}, device_id_type=MESH,
        )

    def prop_to_next(row):
        return pltpu.make_async_remote_copy(
            prop_send.at[row], arrived.at[row], tm_send.at[2 + row], tm_recv.at[2 + row],
            device_id={"tm": tm + 1}, device_id_type=MESH,
        )

    for load in loads[:4]:
        load.wait()
    for row in range(2):
        for at, size in CHUNKS:
            rows = pl.ds(at, size)
            dual = lam[row, rows, :]
            product_now = spread[row, rows, :] * dual
            lam_send[row, rows, :] = dual.astype(BF16)
            i6[2 + row, rows, :] = incr[row, rows, :].astype(BF16)
            scaled[row, rows, :] = product_now
            s6[2 + row, rows, :] = product_now.astype(BF16)

    @pl.when(jnp.logical_not(has_dn))
    def _():
        w3[0] = jnp.zeros_like(w3[0])
        for buffer in (i6, l6, s6):
            for row in (0, 1):
                buffer[row] = jnp.zeros_like(buffer[row])

    @pl.when(jnp.logical_not(has_up))
    def _():
        w3[2] = jnp.zeros_like(w3[2])
        for buffer in (i6, l6, s6):
            for row in (4, 5):
                buffer[row] = jnp.zeros_like(buffer[row])

    @pl.when(jnp.logical_not(has_prev))
    def _():
        arrived[...] = jnp.zeros_like(arrived)

    pl.semaphore_wait(barrier, targets)

    @pl.when(has_prev)
    def _():
        dual_to_prev(0).start()
        dual_to_prev(1).start()

    start_lat([WIN, INC, INC + 1], has_next)
    loads[4].wait()
    edges = [MEM, MEM + 1, DUAL]
    start_lat(edges, sides=(True,))
    start_lat([SCA, SCA + 1])
    for up in (True, False):

        @pl.when(sends_dual(up))
        def _():
            for row in range(2):
                dual_across(row, up).start()

    for load in loads[5:]:
        load.wait()
    mats[0], mats[1] = split(mixing[...])
    mats[2], mats[3] = split(mixing[...].T)
    high, low = split(vert[...])
    high_t, low_t = split(vert[...].T)
    mats[4], mats[5] = split(dot(high, high_t) + (dot(high, low_t) + dot(low, high_t)))

    for at, size in CHUNKS:
        rows = pl.ds(at, size)
        totals = [None, None]
        duals = [lam[row, rows, :] for row in range(2)]
        for m in range(NENS):
            perturb = [members[row, m, rows, :].astype(F32) for row in range(2)]
            weighted = [perturb[row] * duals[row] for row in range(2)]
            for row in range(2):
                near = weighted[1 - row] + east_of(weighted[row]) + west_of(weighted[row])
                term = perturb[row] * (weighted[row] + 0.25 * near)
                totals[row] = term if m == 0 else totals[row] + term
        for row in range(2):
            ens[row, rows, :] = (0.5 / (NENS - 1)) * totals[row] + incr[row, rows, :]

    start_lat(edges, sides=(False,))
    def dual_row(row, cond=True):
        @pl.when(has_next & cond)
        def _():
            dual_to_prev(row).wait_recv()

        start_lat([LNX + row], has_next & cond)

    pass_on(edges, ("seven",), (True,))
    pass_on([SCA, SCA + 1], ("seven",))
    pass_duals()
    for row in range(2):
        dual_row(row, first_duals)

    def weights(i):
        block, row = (i + 2) // 2, (i + 2) % 2
        north, south, east, west = (w3[block, p, row : row + 1, :] for p in range(4))
        return north, south, east, west, 1.0 - north - south - east - west

    low_edge = jnp.where(has_dn, 1.0, 0.0).astype(F32)
    high_edge = jnp.where(has_up, 1.0, 0.0).astype(F32)

    def inside(i, value):
        if i == -1:
            return value * low_edge
        if i == 2:
            return value * high_edge
        return value

    @pl.when(has_next)
    def _():
        await_lat([WIN, INC, INC + 1])

        def transport(of, i, rows):
            north, south, east, west, centre = weights(i)
            here = of(i, rows)
            total = centre * here + north * of(i + 1, rows) + south * of(i - 1, rows)
            return total + east * east_of(here) + west * west_of(here)

        def first(i, rows):
            if 0 <= i < 2:
                return incr[i, rows, :]
            return i6[i + 2, rows, :].astype(F32)

        for i in range(-1, 3):
            for at, size in CHUNKS:
                rows = pl.ds(at, size)
                za[i + 1, rows, :] = inside(i, transport(first, i, rows))
        for i in range(4):
            zb[i] = product(mats, 0, za[i])
        for i in range(2):
            for at, size in CHUNKS:
                rows = pl.ds(at, size)
                za[i, rows, :] = transport(lambda j, r: zb[j + 1, r, :], i, rows)
        for i in range(2):
            prop_send[i] = product(mats, 0, za[i]).astype(BF16)
            prop_to_next(i).start()

    pass_on(edges, ("six",))
    dual_row(0, jnp.logical_not(first_duals))
    pass_on(edges, ("one",))
    pass_on([SCA, SCA + 1], ("one",))
    dual_row(1, jnp.logical_not(first_duals))
    pass_on(edges, ("seven",), (False,))

    scale = 0.5 * 0.25 / (NENS - 1)

    def edge_products(from_below, cond):
        has = (has_dn if from_below else has_up) & cond
        row, side, half = (0, 0, pl.ds(0, HALF)) if from_below else (1, 1, pl.ds(HALF, HALF))

        @pl.when(has)
        def _():
            for item in edges:
                to_lat(item, from_below).wait_recv()
            for at, size in CHUNKS:
                rows = pl.ds(at, size)
                both = None
                for m in range(NENS):
                    term = members[row, m, rows, half].astype(F32) * p_recv[side, m, rows, :].astype(F32)
                    both = term if m == 0 else both + term
                ens[row, rows, half] += scale * (both * d_recv[side, rows, :].astype(F32))
                b_send[row, rows, :] = (both * lam[row, rows, half]).astype(BF16)
            to_lat(BACK, not from_below).start()

    def add_back():
        await_lat([BACK])
        for from_below, has in ((True, has_dn), (False, has_up)):
            row, side, half = (0, 0, pl.ds(HALF, HALF)) if from_below else (1, 1, pl.ds(0, HALF))

            @pl.when(has)
            def _():
                for at, size in CHUNKS:
                    rows = pl.ds(at, size)
                    ens[row, rows, half] += scale * b_recv[side, rows, :].astype(F32)

    edge_products(True, jnp.logical_not(cross_dn))
    edge_products(False, jnp.logical_not(cross_up))

    @pl.when(has_next)
    def _():
        for i in (2, 3):
            ya[i] = product_16(mats, 2, l6[i])

    edge_products(True, cross_dn)
    edge_products(False, cross_up)

    await_lat([SCA, SCA + 1])

    def smooth(of, i, rows):
        here = of(i, rows)
        return here + 0.25 * (of(i + 1, rows) + of(i - 1, rows) + east_of(here) + west_of(here))

    def field(i, rows):
        if 0 <= i < 2:
            return scaled[i, rows, :]
        return s6[i + 2, rows, :].astype(F32)

    for i in range(-1, 3):
        for at, size in CHUNKS:
            rows = pl.ds(at, size)
            za[i + 1, rows, :] = inside(i, smooth(field, i, rows))
    for i in range(2):
        for at, size in CHUNKS:
            rows = pl.ds(at, size)
            zb[i, rows, :] = smooth(lambda j, r: za[j + 1, r, :], i, rows)
    for i in range(2):
        za[i] = product(mats, 4, zb[i])
        for at, size in CHUNKS:
            rows = pl.ds(at, size)
            ens[i, rows, :] += 0.5 * (spread[i, rows, :] * za[i, rows, :])

    @pl.when(has_next)
    def _():
        await_lat([LNX, LNX + 1])

        def transport_back(of, i, rows):
            _, _, east, west, centre = weights(i)
            north, south = weights(i - 1)[0], weights(i + 1)[1]
            here = of(i, rows)
            total = centre * here + north * of(i - 1, rows) + south * of(i + 1, rows)
            return total + west_of(east * here) + east_of(west * here)

        for i in (0, 1, 4, 5):
            ya[i] = product_16(mats, 2, l6[i])
        for i in range(-1, 3):
            for at, size in CHUNKS:
                rows = pl.ds(at, size)
                za[i + 1, rows, :] = inside(
                    i, transport_back(lambda j, r: ya[j + 2, r, :], i, rows)
                )
        for i in range(4):
            zb[i] = product(mats, 2, za[i])
        for i in range(2):
            for at, size in CHUNKS:
                rows = pl.ds(at, size)
                back = transport_back(lambda j, r: zb[j + 1, r, :], i, rows)
                incr_out[i, rows, :] = lam[i, rows, :] - back

    @pl.when(jnp.logical_not(has_next))
    def _():
        incr_out[...] = lam[...]

    add_back()

    @pl.when(has_prev)
    def _():
        prop_from = [
            pltpu.make_async_remote_copy(
                prop_send.at[row], arrived.at[row], tm_send.at[2 + row], tm_recv.at[2 + row],
                device_id={"tm": tm - 1}, device_id_type=MESH,
            )
            for row in range(2)
        ]
        for copy in prop_from:
            copy.wait_recv()

    for i in range(2):
        for at, size in CHUNKS:
            rows = pl.ds(at, size)
            lam_out[i, rows, :] = ens[i, rows, :] - arrived[i, rows, :].astype(F32)

    @pl.when(has_prev)
    def _():
        dual_to_prev(0).wait_send()
        dual_to_prev(1).wait_send()

    @pl.when(has_next)
    def _():
        prop_to_next(0).wait_send()
        prop_to_next(1).wait_send()

    for up, has, cross in ((True, has_up, cross_up), (False, has_dn, cross_dn)):

        @pl.when(has)
        def _():
            for item in [SCA, SCA + 1, *edges, BACK]:
                to_lat(item, up).wait_send()

        @pl.when(has & has_next)
        def _():
            for item in [WIN, INC, INC + 1]:
                to_lat(item, up).wait_send()

        @pl.when(has & has_next & (jnp.logical_not(cross) | jnp.logical_not(straight(up))))
        def _():
            for item in [LNX, LNX + 1]:
                to_lat(item, up).wait_send()

        @pl.when(sends_dual(up))
        def _():
            for row in range(2):
                dual_across(row, up).wait_send()

        for kind, even in RELAYS:

            @pl.when(passes(kind, even, up))
            def _():
                for at, item in enumerate(ROUTES[even][kind]):
                    from_fwd(item, kind, at, up).wait_send()

        @pl.when(passes_dual(up))
        def _():
            for row in range(2):
                from_fwd(LNX + row, "seven", FAR + row, up).wait_send()


def per_device(lam, incr, winds, mixing, spread, vert_corr, members):
    row = (COMP, LON)
    vmem = pl.BlockSpec(memory_space=pltpu.VMEM)
    state = jax.ShapeDtypeStruct((2, *row), F32)
    dma = pltpu.SemaphoreType.DMA
    scratch = [
        pltpu.VMEM((2, *row), F32),
        pltpu.VMEM((2, *row), F32),
        pltpu.VMEM((COMP, COMP), F32),
        pltpu.VMEM((2, *row), F32),
        pltpu.VMEM((COMP, COMP), F32),
        pltpu.VMEM((2, NENS, *row), BF16),
        pltpu.VMEM((6, *row), BF16),
        pltpu.VMEM((6, *row), BF16),
        pltpu.VMEM((6, *row), BF16),
        pltpu.VMEM((3, 4, 2, LON), F32),
        pltpu.VMEM((2, NENS, COMP, HALF), BF16),
        pltpu.VMEM((2, COMP, HALF), BF16),
        pltpu.VMEM((2, COMP, HALF), BF16),
        pltpu.VMEM((2, COMP, HALF), BF16),
        pltpu.VMEM((2, *row), BF16),
        pltpu.VMEM((2, *row), BF16),
        pltpu.VMEM((2, *row), BF16),
        pltpu.VMEM((SLOTS, *row), BF16),
        pltpu.VMEM((2, 2, COMP, HALF), BF16),
        pltpu.VMEM((COMP, HALF), BF16),
        pltpu.VMEM((6, COMP, COMP), BF16),
        pltpu.VMEM((2, *row), F32),
        pltpu.VMEM((6, *row), F32),
        pltpu.VMEM((4, *row), F32),
        pltpu.VMEM((4, *row), F32),
        pltpu.VMEM((2, *row), F32),
        dma((7,)),
        dma((4,)),
        dma((4,)),
        dma((ITEMS,)),
        dma((ITEMS,)),
        dma((ITEMS,)),
        dma((ITEMS,)),
        dma((SLOTS,)),
        dma((SLOTS,)),
        dma((2,)),
    ]
    lam_result, incr_result = pl.pallas_call(
        kernel,
        out_shape=(state, state),
        in_specs=[pl.BlockSpec(memory_space=pltpu.HBM)] * 7,
        out_specs=(vmem, vmem),
        scratch_shapes=scratch,
        compiler_params=pltpu.CompilerParams(
            collective_id=0, has_side_effects=True, vmem_limit_bytes=48 * 2**20
        ),
    )(
        *(
            pltpu.with_memory_space_constraint(array, pltpu.HBM)
            for array in (lam[0], incr[0], winds[0], mixing[0], spread[0], vert_corr, members[0])
        )
    )
    return lam_result[None], incr_result[None]


def solution(mesh):
    in_specs = (
        P("tm", "lat", None, None),
        P("tm", "lat", None, None),
        P("tm", None, "lat", None),
        P("tm", None, None),
        P("tm", "lat", None, None),
        P(),
        P("tm", "lat", None, None, None),
    )
    out_specs = (P("tm", "lat", None, None), P("tm", "lat", None, None))
    return jax.shard_map(
        per_device, mesh=mesh, in_specs=in_specs, out_specs=out_specs, check_vma=False
    )
```

```python
import jax
import jax.numpy as jnp
from jax import lax
from jax.experimental import pallas as pl
from jax.experimental.pallas import tpu as pltpu
from jax.sharding import PartitionSpec as P

MESH = pl.DeviceIdType.MESH
F32, BF16 = jnp.float32, jnp.bfloat16
COMP, LON, NENS = 216, 256, 4
HALF = LON // 2
TM, LAT, BAND = 8, 64, 16
CHUNKS = [(at, min(32, COMP - at)) for at in range(0, COMP, 32)]

WIN, INC, SCA, LNX, MEM, DUAL, BACK = 0, 1, 3, 5, 7, 9, 10
ITEMS = 11
PLACES = {"seven": 14, "six": 12, "one": 2}
ROUTES = {
    True: {"seven": (SCA, MEM), "six": (SCA + 1, MEM + 1, DUAL)},
    False: {"seven": (MEM,), "one": (SCA, SCA + 1, MEM + 1, DUAL)},
}
RELAYS = [(kind, even) for even, kinds in ROUTES.items() for kind in kinds]
FAR = 4
SLOTS = FAR + 2


def route(item, even):
    for kind, items in ROUTES[even].items():
        if item in items:
            return kind, items.index(item)
    return None


def split(value):
    high = value.astype(BF16)
    return high, (value - high.astype(F32)).astype(BF16)


def dot(a, b):
    return jnp.dot(a, b, preferred_element_type=F32)


def product(mats, base, value):
    high, low = split(value)
    return dot(mats[base], high) + (dot(mats[base + 1], high) + dot(mats[base], low))


def product_16(mats, base, value):
    return dot(mats[base], value) + dot(mats[base + 1], value)


def east_of(value):
    return pltpu.roll(value, LON - 1, 1)


def west_of(value):
    return pltpu.roll(value, 1, 1)


def kernel(
    lam_hbm, incr_hbm, winds_hbm, mixing_hbm, spread_hbm, vert_hbm, members_hbm, lam_out, incr_out,
    lam, incr, mixing, spread, vert, members,
    i6, l6, s6, w3, p_recv, d_recv, b_send, b_recv, lam_send, prop_send, arrived, fwd, fwd_p, fwd_d,
    mats, scaled, ya, za, zb, ens,
    load_sem, tm_send, tm_recv, up_send, up_recv, dn_send, dn_recv, f_in, f_out, far_send,
):
    tm, lat = lax.axis_index("tm"), lax.axis_index("lat")
    place = lax.rem(lat, BAND)
    has_up, has_dn = lat < LAT - 1, lat > 0
    has_next, has_prev = tm < TM - 1, tm > 0
    cross_up = (place == BAND - 1) & has_up
    cross_dn = (place == 0) & has_dn

    is_even = lax.rem(tm, 2) == 0
    is_odd = jnp.logical_not(is_even)

    def at_place(kind, up):
        if up:
            return (place == PLACES[kind]) & (lat >= BAND)
        return (place == BAND - 1 - PLACES[kind]) & (lat < LAT - BAND)

    def of_tm(even):
        return is_even if even else is_odd

    def passes(kind, even, up):
        return at_place(kind, up) & of_tm(even)

    def straight(up):
        return is_even if up else is_odd

    def passes_dual(up):
        return at_place("seven", up) & straight(up) & has_next

    first_duals = (cross_up & is_odd) | (cross_dn & is_even)

    def sends_dual(up):
        return (cross_up if up else cross_dn) & jnp.logical_not(straight(up)) & has_prev

    barrier = pltpu.get_barrier_semaphore()
    greetings = [
        (has_next, {"tm": tm + 1}, has_prev),
        (has_prev, {"tm": tm - 1}, has_next),
        (has_up, {"lat": lat + 1}, has_dn),
        (has_dn, {"lat": lat - 1}, has_up),
        (passes_dual(True), {"tm": tm + 1, "lat": lat - PLACES["seven"] - 1}, sends_dual(True)),
        (passes_dual(False), {"tm": tm + 1, "lat": lat + PLACES["seven"] + 1}, sends_dual(False)),
    ]
    for kind, even in RELAYS:
        p = PLACES[kind]
        greetings += [
            (cross_up & of_tm(even), {"lat": lat - p}, passes(kind, even, False)),
            (cross_dn & of_tm(even), {"lat": lat + p}, passes(kind, even, True)),
            (passes(kind, even, True), {"lat": lat - p - 1}, cross_up & of_tm(even)),
            (passes(kind, even, False), {"lat": lat + p + 1}, cross_dn & of_tm(even)),
        ]
    targets = 0
    for cond, where, mirrored in greetings:
        targets = targets + jnp.where(mirrored, 1, 0)

        @pl.when(cond)
        def _():
            pl.semaphore_signal(barrier, inc=1, device_id=where, device_id_type=MESH)

    loads = [
        pltpu.make_async_copy(src, dst, load_sem.at[at])
        for at, (src, dst) in enumerate(
            (
                (lam_hbm, lam),
                (spread_hbm, spread),
                (incr_hbm, incr),
                (winds_hbm, w3.at[1]),
                (members_hbm, members),
                (mixing_hbm, mixing),
                (vert_hbm, vert),
            )
        )
    ]
    for load in loads:
        load.start()

    def ends(item, up):
        if item == WIN:
            return w3.at[1], w3.at[0 if up else 2]
        for first, buffer in ((INC, i6), (SCA, s6), (LNX, l6)):
            if first <= item < first + 2:
                row = item - first
                return buffer.at[2 + row], buffer.at[row if up else 4 + row]
        row, side, half = (1, 0, pl.ds(0, HALF)) if up else (0, 1, pl.ds(HALF, HALF))
        if item == DUAL:
            return lam_send.at[row, :, half], d_recv.at[side]
        if item == BACK:
            return b_send.at[row], b_recv.at[side]
        pair = pl.ds(2 * (item - MEM), 2)
        return members.at[row, pair, :, half], p_recv.at[side, pair]

    def slot(item, at):
        if item in (MEM, MEM + 1):
            return fwd_p.at[item - MEM]
        return fwd_d if item == DUAL else fwd.at[at]

    def to_lat(item, up):
        src, dst = ends(item, up)
        send, recv = (up_send, up_recv) if up else (dn_send, dn_recv)
        where = {"lat": lat + 1 if up else lat - 1}
        return pltpu.make_async_remote_copy(
            src, dst, send.at[item], recv.at[item], device_id=where, device_id_type=MESH
        )

    def dual_across(row, up):
        where = {"tm": tm - 1, "lat": lat + BAND - 1 if up else lat - BAND + 1}
        return pltpu.make_async_remote_copy(
            lam_send.at[row], fwd.at[FAR + row], far_send.at[row], f_in.at[FAR + row],
            device_id=where, device_id_type=MESH,
        )

    def to_fwd(item, up, even):
        src, _ = ends(item, up)
        kind, at = route(item, even)
        send = up_send if up else dn_send
        p = PLACES[kind]
        where = {"lat": lat + p + 1 if up else lat - p - 1}
        return pltpu.make_async_remote_copy(
            src, slot(item, at), send.at[item], f_in.at[at], device_id=where, device_id_type=MESH
        )

    def from_fwd(item, kind, at, up):
        _, dst = ends(item, up)
        recv = up_recv if up else dn_recv
        p = PLACES[kind]
        where = {"lat": lat - p if up else lat + p}
        return pltpu.make_async_remote_copy(
            slot(item, at), dst, f_out.at[at], recv.at[item], device_id=where, device_id_type=MESH
        )

    def start_lat(items, cond=True, sides=(True, False)):
        for up, has, cross in ((True, has_up, cross_up), (False, has_dn, cross_dn)):
            if False in sides:

                @pl.when(has & jnp.logical_not(cross) & cond)
                def _():
                    for item in items:
                        to_lat(item, up).start()

            if True not in sides:
                continue
            for even in (True, False):

                @pl.when(cross & (is_even if even else is_odd) & cond)
                def _():
                    for item in items:
                        if route(item, even):
                            to_fwd(item, up, even).start()
                        elif item not in (LNX, LNX + 1) or even != up:
                            to_lat(item, up).start()

    def hand_over(item, kind, at, up):
        pltpu.make_async_remote_copy(
            slot(item, at), slot(item, at), f_out.at[at], f_in.at[at],
            device_id={"lat": lat - 1 if up else lat + 1}, device_id_type=MESH,
        ).wait_recv()
        from_fwd(item, kind, at, up).start()

    def pass_on(items, kinds, parities=(True, False)):
        for kind, even in RELAYS:
            if kind not in kinds or even not in parities:
                continue
            now = [item for item in items if item in ROUTES[even][kind]]
            if not now:
                continue
            for up in (True, False):

                @pl.when(passes(kind, even, up))
                def _():
                    for item in now:
                        hand_over(item, kind, route(item, even)[1], up)

    def pass_duals():
        for up in (True, False):

            @pl.when(passes_dual(up))
            def _():
                for row in range(2):
                    hand_over(LNX + row, "seven", FAR + row, up)

    def await_lat(items, cond=True):
        for up, has in ((True, has_dn), (False, has_up)):

            @pl.when(has & cond)
            def _():
                for item in items:
                    to_lat(item, up).wait_recv()

    def dual_to_prev(row):
        return pltpu.make_async_remote_copy(
            lam_send.at[row], l6.at[2 + row], tm_send.at[row], tm_recv.at[row],
            device_id={"tm": tm - 1}, device_id_type=MESH,
        )

    def prop_to_next(row):
        return pltpu.make_async_remote_copy(
            prop_send.at[row], arrived.at[row], tm_send.at[2 + row], tm_recv.at[2 + row],
            device_id={"tm": tm + 1}, device_id_type=MESH,
        )

    for load in loads[:4]:
        load.wait()
    for row in range(2):
        for at, size in CHUNKS:
            rows = pl.ds(at, size)
            dual = lam[row, rows, :]
            product_now = spread[row, rows, :] * dual
            lam_send[row, rows, :] = dual.astype(BF16)
            i6[2 + row, rows, :] = incr[row, rows, :].astype(BF16)
            scaled[row, rows, :] = product_now
            s6[2 + row, rows, :] = product_now.astype(BF16)

    @pl.when(jnp.logical_not(has_dn))
    def _():
        w3[0] = jnp.zeros_like(w3[0])
        for buffer in (i6, l6, s6):
            for row in (0, 1):
                buffer[row] = jnp.zeros_like(buffer[row])

    @pl.when(jnp.logical_not(has_up))
    def _():
        w3[2] = jnp.zeros_like(w3[2])
        for buffer in (i6, l6, s6):
            for row in (4, 5):
                buffer[row] = jnp.zeros_like(buffer[row])

    @pl.when(jnp.logical_not(has_prev))
    def _():
        arrived[...] = jnp.zeros_like(arrived)

    pl.semaphore_wait(barrier, targets)

    @pl.when(has_prev)
    def _():
        dual_to_prev(0).start()
        dual_to_prev(1).start()

    start_lat([WIN, INC, INC + 1], has_next)
    loads[4].wait()
    edges = [MEM, MEM + 1, DUAL]
    start_lat(edges, sides=(True,))
    start_lat([SCA, SCA + 1])
    for up in (True, False):

        @pl.when(sends_dual(up))
        def _():
            for row in range(2):
                dual_across(row, up).start()

    for load in loads[5:]:
        load.wait()
    mats[0], mats[1] = split(mixing[...])
    mats[2], mats[3] = split(mixing[...].T)
    high, low = split(vert[...])
    high_t, low_t = split(vert[...].T)
    mats[4], mats[5] = split(dot(high, high_t) + (dot(high, low_t) + dot(low, high_t)))

    for at, size in CHUNKS:
        rows = pl.ds(at, size)
        totals = [None, None]
        duals = [lam[row, rows, :] for row in range(2)]
        for m in range(NENS):
            perturb = [members[row, m, rows, :].astype(F32) for row in range(2)]
            weighted = [perturb[row] * duals[row] for row in range(2)]
            for row in range(2):
                near = weighted[1 - row] + east_of(weighted[row]) + west_of(weighted[row])
                term = perturb[row] * (weighted[row] + 0.25 * near)
                totals[row] = term if m == 0 else totals[row] + term
        for row in range(2):
            ens[row, rows, :] = (0.5 / (NENS - 1)) * totals[row] + incr[row, rows, :]

    start_lat(edges, sides=(False,))
    def dual_row(row, cond=True):
        @pl.when(has_next & cond)
        def _():
            dual_to_prev(row).wait_recv()

        start_lat([LNX + row], has_next & cond)

    pass_on(edges, ("seven",), (True,))
    pass_duals()
    pass_on([SCA, SCA + 1], ("seven",))
    for row in range(2):
        dual_row(row, first_duals)

    def weights(i):
        block, row = (i + 2) // 2, (i + 2) % 2
        north, south, east, west = (w3[block, p, row : row + 1, :] for p in range(4))
        return north, south, east, west, 1.0 - north - south - east - west

    low_edge = jnp.where(has_dn, 1.0, 0.0).astype(F32)
    high_edge = jnp.where(has_up, 1.0, 0.0).astype(F32)

    def inside(i, value):
        if i == -1:
            return value * low_edge
        if i == 2:
            return value * high_edge
        return value

    @pl.when(has_next)
    def _():
        await_lat([WIN, INC, INC + 1])

        def transport(of, i, rows):
            north, south, east, west, centre = weights(i)
            here = of(i, rows)
            total = centre * here + north * of(i + 1, rows) + south * of(i - 1, rows)
            return total + east * east_of(here) + west * west_of(here)

        def first(i, rows):
            if 0 <= i < 2:
                return incr[i, rows, :]
            return i6[i + 2, rows, :].astype(F32)

        for i in range(-1, 3):
            for at, size in CHUNKS:
                rows = pl.ds(at, size)
                za[i + 1, rows, :] = inside(i, transport(first, i, rows))
        for i in range(4):
            zb[i] = product(mats, 0, za[i])
        for i in range(2):
            for at, size in CHUNKS:
                rows = pl.ds(at, size)
                za[i, rows, :] = transport(lambda j, r: zb[j + 1, r, :], i, rows)
        for i in range(2):
            prop_send[i] = product(mats, 0, za[i]).astype(BF16)
            prop_to_next(i).start()

    pass_on(edges, ("six",))
    pass_on([SCA + 1], ("six",))
    dual_row(0, jnp.logical_not(first_duals))
    pass_on(edges, ("one",))
    pass_on([SCA, SCA + 1], ("one",))
    dual_row(1, jnp.logical_not(first_duals))
    pass_on(edges, ("seven",), (False,))

    scale = 0.5 * 0.25 / (NENS - 1)

    def edge_products(from_below, cond):
        has = (has_dn if from_below else has_up) & cond
        row, side, half = (0, 0, pl.ds(0, HALF)) if from_below else (1, 1, pl.ds(HALF, HALF))

        @pl.when(has)
        def _():
            for item in edges:
                to_lat(item, from_below).wait_recv()
            for at, size in CHUNKS:
                rows = pl.ds(at, size)
                both = None
                for m in range(NENS):
                    term = members[row, m, rows, half].astype(F32) * p_recv[side, m, rows, :].astype(F32)
                    both = term if m == 0 else both + term
                ens[row, rows, half] += scale * (both * d_recv[side, rows, :].astype(F32))
                b_send[row, rows, :] = (both * lam[row, rows, half]).astype(BF16)
            to_lat(BACK, not from_below).start()

    def add_back():
        await_lat([BACK])
        for from_below, has in ((True, has_dn), (False, has_up)):
            row, side, half = (0, 0, pl.ds(HALF, HALF)) if from_below else (1, 1, pl.ds(0, HALF))

            @pl.when(has)
            def _():
                for at, size in CHUNKS:
                    rows = pl.ds(at, size)
                    ens[row, rows, half] += scale * b_recv[side, rows, :].astype(F32)

    edge_products(True, jnp.logical_not(cross_dn))
    edge_products(False, jnp.logical_not(cross_up))

    @pl.when(has_next)
    def _():
        for i in (2, 3):
            ya[i] = product_16(mats, 2, l6[i])

    edge_products(True, cross_dn)
    edge_products(False, cross_up)

    await_lat([SCA, SCA + 1])

    def smooth(of, i, rows):
        here = of(i, rows)
        return here + 0.25 * (of(i + 1, rows) + of(i - 1, rows) + east_of(here) + west_of(here))

    def field(i, rows):
        if 0 <= i < 2:
            return scaled[i, rows, :]
        return s6[i + 2, rows, :].astype(F32)

    for i in range(-1, 3):
        for at, size in CHUNKS:
            rows = pl.ds(at, size)
            za[i + 1, rows, :] = inside(i, smooth(field, i, rows))
    for i in range(2):
        for at, size in CHUNKS:
            rows = pl.ds(at, size)
            zb[i, rows, :] = smooth(lambda j, r: za[j + 1, r, :], i, rows)
    for i in range(2):
        za[i] = product(mats, 4, zb[i])
        for at, size in CHUNKS:
            rows = pl.ds(at, size)
            ens[i, rows, :] += 0.5 * (spread[i, rows, :] * za[i, rows, :])

    @pl.when(has_next)
    def _():
        await_lat([LNX, LNX + 1])

        def transport_back(of, i, rows):
            _, _, east, west, centre = weights(i)
            north, south = weights(i - 1)[0], weights(i + 1)[1]
            here = of(i, rows)
            total = centre * here + north * of(i - 1, rows) + south * of(i + 1, rows)
            return total + west_of(east * here) + east_of(west * here)

        for i in (0, 1, 4, 5):
            ya[i] = product_16(mats, 2, l6[i])
        for i in range(-1, 3):
            for at, size in CHUNKS:
                rows = pl.ds(at, size)
                za[i + 1, rows, :] = inside(
                    i, transport_back(lambda j, r: ya[j + 2, r, :], i, rows)
                )
        for i in range(4):
            zb[i] = product(mats, 2, za[i])
        for i in range(2):
            for at, size in CHUNKS:
                rows = pl.ds(at, size)
                back = transport_back(lambda j, r: zb[j + 1, r, :], i, rows)
                incr_out[i, rows, :] = lam[i, rows, :] - back

    @pl.when(jnp.logical_not(has_next))
    def _():
        incr_out[...] = lam[...]

    add_back()

    @pl.when(has_prev)
    def _():
        prop_from = [
            pltpu.make_async_remote_copy(
                prop_send.at[row], arrived.at[row], tm_send.at[2 + row], tm_recv.at[2 + row],
                device_id={"tm": tm - 1}, device_id_type=MESH,
            )
            for row in range(2)
        ]
        for copy in prop_from:
            copy.wait_recv()

    for i in range(2):
        for at, size in CHUNKS:
            rows = pl.ds(at, size)
            lam_out[i, rows, :] = ens[i, rows, :] - arrived[i, rows, :].astype(F32)

    @pl.when(has_prev)
    def _():
        dual_to_prev(0).wait_send()
        dual_to_prev(1).wait_send()

    @pl.when(has_next)
    def _():
        prop_to_next(0).wait_send()
        prop_to_next(1).wait_send()

    for up, has, cross in ((True, has_up, cross_up), (False, has_dn, cross_dn)):

        @pl.when(has)
        def _():
            for item in [SCA, SCA + 1, *edges, BACK]:
                to_lat(item, up).wait_send()

        @pl.when(has & has_next)
        def _():
            for item in [WIN, INC, INC + 1]:
                to_lat(item, up).wait_send()

        @pl.when(has & has_next & (jnp.logical_not(cross) | jnp.logical_not(straight(up))))
        def _():
            for item in [LNX, LNX + 1]:
                to_lat(item, up).wait_send()

        @pl.when(sends_dual(up))
        def _():
            for row in range(2):
                dual_across(row, up).wait_send()

        for kind, even in RELAYS:

            @pl.when(passes(kind, even, up))
            def _():
                for at, item in enumerate(ROUTES[even][kind]):
                    from_fwd(item, kind, at, up).wait_send()

        @pl.when(passes_dual(up))
        def _():
            for row in range(2):
                from_fwd(LNX + row, "seven", FAR + row, up).wait_send()


def per_device(lam, incr, winds, mixing, spread, vert_corr, members):
    row = (COMP, LON)
    vmem = pl.BlockSpec(memory_space=pltpu.VMEM)
    state = jax.ShapeDtypeStruct((2, *row), F32)
    dma = pltpu.SemaphoreType.DMA
    scratch = [
        pltpu.VMEM((2, *row), F32),
        pltpu.VMEM((2, *row), F32),
        pltpu.VMEM((COMP, COMP), F32),
        pltpu.VMEM((2, *row), F32),
        pltpu.VMEM((COMP, COMP), F32),
        pltpu.VMEM((2, NENS, *row), BF16),
        pltpu.VMEM((6, *row), BF16),
        pltpu.VMEM((6, *row), BF16),
        pltpu.VMEM((6, *row), BF16),
        pltpu.VMEM((3, 4, 2, LON), F32),
        pltpu.VMEM((2, NENS, COMP, HALF), BF16),
        pltpu.VMEM((2, COMP, HALF), BF16),
        pltpu.VMEM((2, COMP, HALF), BF16),
        pltpu.VMEM((2, COMP, HALF), BF16),
        pltpu.VMEM((2, *row), BF16),
        pltpu.VMEM((2, *row), BF16),
        pltpu.VMEM((2, *row), BF16),
        pltpu.VMEM((SLOTS, *row), BF16),
        pltpu.VMEM((2, 2, COMP, HALF), BF16),
        pltpu.VMEM((COMP, HALF), BF16),
        pltpu.VMEM((6, COMP, COMP), BF16),
        pltpu.VMEM((2, *row), F32),
        pltpu.VMEM((6, *row), F32),
        pltpu.VMEM((4, *row), F32),
        pltpu.VMEM((4, *row), F32),
        pltpu.VMEM((2, *row), F32),
        dma((7,)),
        dma((4,)),
        dma((4,)),
        dma((ITEMS,)),
        dma((ITEMS,)),
        dma((ITEMS,)),
        dma((ITEMS,)),
        dma((SLOTS,)),
        dma((SLOTS,)),
        dma((2,)),
    ]
    lam_result, incr_result = pl.pallas_call(
        kernel,
        out_shape=(state, state),
        in_specs=[pl.BlockSpec(memory_space=pltpu.HBM)] * 7,
        out_specs=(vmem, vmem),
        scratch_shapes=scratch,
        compiler_params=pltpu.CompilerParams(
            collective_id=0, has_side_effects=True, vmem_limit_bytes=48 * 2**20
        ),
    )(
        *(
            pltpu.with_memory_space_constraint(array, pltpu.HBM)
            for array in (lam[0], incr[0], winds[0], mixing[0], spread[0], vert_corr, members[0])
        )
    )
    return lam_result[None], incr_result[None]


def solution(mesh):
    in_specs = (
        P("tm", "lat", None, None),
        P("tm", "lat", None, None),
        P("tm", None, "lat", None),
        P("tm", None, None),
        P("tm", "lat", None, None),
        P(),
        P("tm", "lat", None, None, None),
    )
    out_specs = (P("tm", "lat", None, None), P("tm", "lat", None, None))
    return jax.shard_map(
        per_device, mesh=mesh, in_specs=in_specs, out_specs=out_specs, check_vma=False
    )
```
